512 devices in a mesh: tm: 512 (over y, x, z, core).
Axes of the slice: x: 4, y: 8, z: 8, core: 2. Of those that a mesh axis runs over, the one named last changes fastest.
Arguments:
- initial: float32 [2, 64, 64], replicated, may hold values from 0 to 0.6
- coarse_guess: float32 [512, 2, 64, 64], P('tm'), may hold values from 0 to 0.6
- feed_rate: float32 [64, 64], replicated, may hold values from 0.02 to 0.08
- kill_rate: float32 [64, 64], replicated, may hold values from 0.03 to 0.07
Outputs:
- trajectory: float32 [2048, 2, 64, 64], P('tm')
- c_residual: float32 [512, 2, 64, 64], P('tm')
- group_coarse: float32 [512, 2, 64, 64], P('tm')
- level_defect: float32 [512, 2, 64, 64], P('tm')
The draws below stay inside these ranges and needn't reach their ends.
All inputs are finite; a program needn't handle non-finite values.
Results may differ from the reference program's by a relative error of at most 0.0004.
Values sent between devices are 32-bit elements; how exact they have to be, the bound alone decides.
No kernel may reach another device: no remote copies, remote signals or barrier semaphores. Data moves between devices by JAX's collectives and lax.ppermute only.
A program may use at most 64 MiB of HBM per device.

```python
import math
import jax
import jax.numpy as jnp
from jax import lax

STEPS_DEV = 4
GX = 64
GY = 64
GROUP = 16
N_TM = 512


def steps_of(stream_key, dims, shards, smallest, top_value):
    def one(position, parts):
        heights = jax.random.uniform(jax.random.fold_in(jax.random.fold_in(stream_key, 6), position), (parts,), jnp.float32, smallest / len(shards), top_value / len(shards))
        return jnp.repeat(jnp.exp(heights), dims[position] // parts).reshape((-1,) + (1,) * (len(dims) - position - 1))

    level = one(*shards[0])
    for cut in shards[1:]:
        level = level * one(*cut)
    return level


def setup_inputs(seed: int = 0) -> dict:
    key_list = jax.random.split(jax.random.key(seed), 5)
    return {
        "initial": jnp.clip(jax.random.uniform(key_list[0], (2, GX, GY), jnp.float32, 0.0, 0.6), 0.0, 0.6),
        "coarse_guess": jnp.clip(0.6 * jax.random.uniform(key_list[1], (N_TM, 2, GX, GY), jnp.float32) ** steps_of(key_list[1], (N_TM, 2, GX, GY), ((0, 512),), -0.2, 0.2), 0.0, 0.6),
        "feed_rate": jnp.clip(jnp.exp(jax.random.uniform(key_list[2], (GX, GY), jnp.float32, math.log(0.02), math.log(0.08))), 0.02, 0.08),
        "kill_rate": jnp.clip(jnp.exp(jax.random.uniform(key_list[3], (GX, GY), jnp.float32, math.log(0.03), math.log(0.07))), 0.03, 0.07),
    }


diffusion = (0.2, 0.1)
interval_time = 0.03125
highest = lax.Precision.HIGHEST

def cosine_basis(length):
    positions = jnp.arange(length, dtype=jnp.float32)
    angles = jnp.pi * (positions[:, None] + 0.5) * positions[None, :] / length
    weight = jnp.where(positions == 0, jnp.sqrt(1.0 / length), jnp.sqrt(2.0 / length))
    return jnp.cos(angles) * weight[None, :]

def eigen_values(length):
    positions = jnp.arange(length, dtype=jnp.float32)
    return -4.0 * jnp.sin(jnp.pi * positions / (2.0 * length)) ** 2

def make_tables(rows_first, rows_second):
    spectrum = eigen_values(rows_first)[:, None] + eigen_values(rows_second)[None, :]
    return (cosine_basis(rows_first), cosine_basis(rows_second), spectrum)

def advance(fields, feed_rate, kill_rate, time_step, tables):
    basis_rows, basis_cols, spectrum = tables
    substrate = fields[..., 0, :, :]
    catalyst = fields[..., 1, :, :]
    uptake = substrate * catalyst * catalyst
    substrate_new = substrate + time_step * (feed_rate * (1.0 - substrate) - uptake)
    catalyst_new = catalyst + time_step * (uptake - (feed_rate + kill_rate) * catalyst)
    reacted = jnp.stack([substrate_new, catalyst_new], axis=-3)
    spectral = jnp.matmul(jnp.matmul(basis_rows.T, reacted, precision=highest), basis_cols, precision=highest)
    diff_rates = jnp.array(diffusion, dtype=jnp.float32)
    spectral = spectral / (1.0 - time_step * diff_rates[:, None, None] * spectrum)
    return jnp.matmul(jnp.matmul(basis_rows, spectral, precision=highest), basis_cols.T, precision=highest)

def march(start_state, feed_rate, kill_rate, time_step, tables, count_steps):

    def turn(fields, unused):
        fields = advance(fields, feed_rate, kill_rate, time_step, tables)
        return (fields, fields)
    finished, visited = lax.scan(turn, start_state, None, length=count_steps)
    return (finished, visited)

def reference(initial, coarse_guess, feed_rate, kill_rate):
    tables = make_tables(initial.shape[1], initial.shape[2])
    fine_step = interval_time / STEPS_DEV
    level_step = interval_time
    coarse_step = interval_time * GROUP
    groups = N_TM // GROUP
    shape = initial.shape

    def before(values):
        return jnp.concatenate([initial[None], values[:-1]], axis=0)

    def evolve(fields, time_step):
        return advance(fields, feed_rate, kill_rate, time_step, tables)
    relaxed, unused = march(before(coarse_guess), feed_rate, kill_rate, fine_step, tables, STEPS_DEV)
    shifted = before(relaxed)
    arrived, unused = march(shifted, feed_rate, kill_rate, fine_step, tables, STEPS_DEV)
    c_residual = arrived - relaxed
    level_rhs = arrived - evolve(shifted, level_step)
    grouped_terms = level_rhs.reshape((groups, GROUP) + shape)
    group_start = jnp.concatenate([initial[None], relaxed.reshape((groups, GROUP) + shape)[:, -1][:-1]], axis=0)

    def level_turn(fields, right_side):
        fields = evolve(fields, level_step) + right_side
        return (fields, fields)
    inner_terms = jnp.moveaxis(grouped_terms[:, :-1], 1, 0)
    last_point, unused = lax.scan(level_turn, group_start, inner_terms)
    closing = evolve(last_point, level_step) + grouped_terms[:, -1]
    coarse_rhs = closing - evolve(group_start, coarse_step)

    def coarse_turn(fields, right_side):
        fields = evolve(fields, coarse_step) + right_side
        return (fields, fields)
    unused, coarse_values = lax.scan(coarse_turn, initial, coarse_rhs)
    group_coarse = jnp.repeat(coarse_values, GROUP, axis=0)
    fresh_start = jnp.concatenate([initial[None], coarse_values[:-1]], axis=0)
    unused, interior = lax.scan(level_turn, fresh_start, inner_terms)
    finishing = evolve(interior[-1], level_step) + grouped_terms[:, -1]
    group_defect = finishing - coarse_values
    level_defect = jnp.concatenate([jnp.zeros((groups, GROUP - 1) + shape, jnp.float32), group_defect[:, None]], axis=1)
    level_defect = level_defect.reshape((N_TM,) + shape)
    corrected = jnp.concatenate([jnp.moveaxis(interior, 0, 1), coarse_values[:, None]], axis=1)
    corrected = corrected.reshape((N_TM,) + shape)
    unused, inside = march(before(corrected), feed_rate, kill_rate, fine_step, tables, STEPS_DEV - 1)
    trajectory = jnp.concatenate([jnp.moveaxis(inside, 0, 1), corrected[:, None]], axis=1)
    return (trajectory.reshape((N_TM * STEPS_DEV,) + shape), c_residual, group_coarse, level_defect)
```

```python
import functools

import jax
import jax.numpy as jnp
import ml_dtypes
import numpy as np
from jax import lax
from jax.experimental import pallas as pl
from jax.experimental.pallas import tpu as pltpu
from jax.sharding import PartitionSpec as P

GRID = 64
GROUP = 16
STEPS_DEV = 4
LANES = 2 * GRID
diffusion = (0.2, 0.1)
interval_time = 0.03125
fine_step = interval_time / STEPS_DEV
level_step = interval_time
coarse_step = interval_time * GROUP


def basis_tables():
    positions = np.arange(GRID, dtype=np.float32)
    angles = np.float32(np.pi) * (positions[:, None] + np.float32(0.5)) * positions[None] / np.float32(GRID)
    weight = np.where(positions == 0, np.sqrt(np.float32(1 / GRID)), np.sqrt(np.float32(2 / GRID)))
    cosines = np.cos(angles.astype(np.float64)).astype(np.float32)
    basis = cosines * weight[None].astype(np.float32)
    sines = np.sin((np.float32(np.pi) * positions / np.float32(2 * GRID)).astype(np.float64)).astype(np.float32)
    return basis.astype(np.float64), (np.float32(-4) * sines * sines).astype(np.float64)


def solve_terms(time_step, rate, rank):
    basis, values = basis_tables()
    inverse = 1 / (1 - time_step * rate * (values[:, None] + values[None]))
    side = inverse[:, 0] - 1
    rest = inverse - 1 - side[:, None] - side[None]
    weights, vectors = np.linalg.eigh(rest)
    order = np.argsort(-np.abs(weights))[:rank]
    first = (basis * side) @ basis.T + basis @ basis.T - np.eye(GRID)
    cross = [(basis * (vectors[:, k] * np.sqrt(np.abs(weights[k])))) @ basis.T for k in order]
    return first, cross, [np.sign(weights[k]) for k in order]


def halves(matrix):
    high = matrix.astype(np.float32).astype(ml_dtypes.bfloat16)
    low = (matrix - high.astype(np.float64)).astype(np.float32).astype(ml_dtypes.bfloat16)
    return high, low


def both(left, right):
    zero = np.zeros((GRID, GRID))
    return np.block([[left, zero], [zero, right]])


@functools.lru_cache(None)
def level_tables(time_step, rank, fine_cross):
    sub_first, sub_cross, sub_sign = solve_terms(time_step, diffusion[0], rank)
    cat_first, cat_cross, cat_sign = solve_terms(time_step, diffusion[1], rank)
    right = [both(sub_first, cat_first)] + [both(a, b) for a, b in zip(sub_cross, cat_cross)]
    high, low = zip(*[halves(m) for m in right])
    right_high = np.concatenate([np.concatenate(high, 1)] * 2, 0)
    right_low = np.concatenate(low if fine_cross else low[:1], 1)
    left_high, left_low = halves(np.concatenate([sub_first, cat_first], 0))
    left_side = np.concatenate([left_high, left_high, left_low], 1)
    stacked = [
        np.concatenate([a * p, b * q], 0) for a, b, p, q in zip(sub_cross, cat_cross, sub_sign, cat_sign)
    ]
    cross_high, cross_low = halves(np.concatenate(stacked, 1))
    tables = [right_high, right_low, left_side, cross_high]
    return tables + ([cross_low] if fine_cross else [])


def product(left, right):
    return jnp.dot(left, right, preferred_element_type=jnp.float32)


def rounded(value):
    high = value.astype(jnp.bfloat16)
    return high, (value - high.astype(jnp.float32)).astype(jnp.bfloat16)


class Level:
    def __init__(self, time_step, rank, fine_cross):
        self.time_step, self.rank, self.fine_cross = time_step, rank, fine_cross
        self.tables = level_tables(time_step, rank, fine_cross)
        self.count = len(self.tables)

    def bind(self, refs, feed, kill):
        tables = [r[...] for r in refs]
        h = jnp.float32(self.time_step)
        second = lax.broadcasted_iota(jnp.int32, (GRID, LANES), 1) >= GRID
        decay = h * jnp.where(second, feed + kill, feed)
        supply = jnp.where(second, jnp.float32(0), h * feed)
        sign = jnp.where(second, h, -h)

        def step(state):
            other = pltpu.roll(state, GRID, 1)
            uptake = state * other * jnp.where(second, state, other)
            reacted = state + (supply - decay * state + sign * uptake)
            high, low = rounded(reacted)
            right = product(jnp.concatenate([high, low], 1), tables[0])
            right_low = product(high, tables[1])
            side = product(tables[2], jnp.concatenate([high, low, high], 0))
            mixed = []
            for k in range(1, self.rank + 1):
                part = right[:, LANES * k : LANES * (k + 1)]
                if self.fine_cross:
                    part = part + right_low[:, LANES * k : LANES * (k + 1)]
                mixed.append(part)
            mixed = jnp.concatenate(mixed, 0)
            if self.fine_cross:
                mixed_high, mixed_low = rounded(mixed)
                cross = product(tables[3], mixed_high) + product(tables[3], mixed_low) + product(tables[4], mixed_high)
            else:
                cross = product(tables[3], mixed.astype(jnp.bfloat16))
            left = side + cross
            left = jnp.where(second, left[GRID:], left[:GRID])
            return reacted + (right[:, :LANES] + right_low[:, :LANES] + left)

        return step


FINE = Level(fine_step, 1, False)
MIDDLE = Level(level_step, 1, True)
COARSE = Level(coarse_step, 3, True)


def packed(pair):
    return jnp.concatenate([pair[0], pair[1]], 1)


def unpack_to(ref, state):
    ref[0] = state[:, :GRID]
    ref[1] = state[:, GRID:]


def steppers(levels, refs, feed_ref, kill_ref):
    feed, kill = packed([feed_ref[...]] * 2), packed([kill_ref[...]] * 2)
    made, start = [], 0
    for level in levels:
        made.append(level.bind(refs[start : start + level.count], feed, kill))
        start += level.count
    return made, refs[start:]


def relax_kernel(near_ref, far_ref, initial_ref, feed_ref, kill_ref, *refs):
    (fine, middle), (share_ref, residual_ref) = steppers([FINE, MIDDLE], refs, feed_ref, kill_ref)
    position = lax.axis_index("tm")
    initial = packed(initial_ref[...])
    own = jnp.where(position == 0, initial, packed(near_ref[...]))
    prior = jnp.where(position == 1, initial, packed(far_ref[...]))

    def relax(turn, states):
        return fine(states[0]), fine(states[1])

    relaxed, shifted = lax.fori_loop(0, STEPS_DEV, relax, (own, prior))
    shifted = jnp.where(position == 0, initial, shifted)
    leap = middle(shifted)
    arrived = lax.fori_loop(0, STEPS_DEV, lambda turn, state: fine(state), shifted)
    share_ref[...] = jnp.where(position % GROUP == 0, shifted, arrived - leap)
    unpack_to(residual_ref, arrived - relaxed)


def group_kernel(shares_ref, feed_ref, kill_ref, *refs):
    (fine, middle, coarse), (first_ref, rhs_ref) = steppers([FINE, MIDDLE, COARSE], refs, feed_ref, kill_ref)
    start = shares_ref[0]
    leap, handed = middle(start), coarse(start)
    state = lax.fori_loop(0, STEPS_DEV, lambda turn, state: fine(state), start)
    first_ref[...] = state - leap
    state = lax.fori_loop(1, GROUP, lambda j, state: middle(state) + shares_ref[j], state)
    leading = lax.axis_index("tm") < GROUP
    rhs_ref[...] = jnp.where(leading, state, state - handed)


def correct_kernel(rhs_ref, shares_ref, first_ref, initial_ref, feed_ref, kill_ref, *refs):
    (fine, middle, coarse), (points_ref, value_ref, defect_ref) = steppers(
        [FINE, MIDDLE, COARSE], refs, feed_ref, kill_ref
    )
    position = lax.axis_index("tm")
    member, group_id = position % GROUP, position // GROUP

    def coarse_turn(g, states):
        return states[1], coarse(states[1]) + rhs_ref[g]

    earlier, value = lax.fori_loop(1, group_id + 1, coarse_turn, (packed(initial_ref[...]), rhs_ref[0]))
    unpack_to(value_ref.at[0], value)

    def right_side(j):
        return jnp.where(j == 0, first_ref[...], shares_ref[j])

    prior = lax.fori_loop(0, member, lambda j, state: middle(state) + right_side(j), earlier)
    updated = middle(prior) + right_side(member)
    closing = member == GROUP - 1
    unpack_to(points_ref.at[STEPS_DEV - 1], jnp.where(closing, value, updated))
    unpack_to(defect_ref.at[0], jnp.where(closing, updated - value, jnp.zeros_like(value)))
    state = prior
    for i in range(STEPS_DEV - 1):
        state = fine(state)
        unpack_to(points_ref.at[i], state)


def call(kernel, shapes, levels, *operands):
    tables = [jnp.asarray(t) for level in levels for t in level.tables]
    where = pl.BlockSpec(memory_space=pltpu.VMEM)
    return pl.pallas_call(
        kernel,
        out_shape=[jax.ShapeDtypeStruct(s, jnp.float32) for s in shapes],
        in_specs=[where] * (len(operands) + len(tables)),
        out_specs=[where] * len(shapes),
        compiler_params=pltpu.CompilerParams(vmem_limit_bytes=48 * 2**20),
    )(*operands, *tables)


def shards(initial, coarse_guess, feed_rate, kill_rate):
    devices = lax.axis_size("tm")
    groups = devices // GROUP
    field = (GRID, LANES)
    pair = (2, GRID, GRID)
    own = coarse_guess[0]
    near = lax.ppermute(own, "tm", [(i, i + 1) for i in range(devices - 1)])
    far = lax.ppermute(own, "tm", [(i, i + 2) for i in range(devices - 2)])
    share, residual = call(
        relax_kernel, [field, pair], [FINE, MIDDLE], near, far, initial, feed_rate, kill_rate
    )
    inside = [[g * GROUP + m for m in range(GROUP)] for g in range(groups)]
    shares = lax.all_gather(share, "tm", axis_index_groups=inside)
    first, rhs = call(group_kernel, [field, field], [FINE, MIDDLE, COARSE], shares, feed_rate, kill_rate)
    across = [[g * GROUP + m for g in range(groups)] for m in range(GROUP)]
    rhs = lax.all_to_all(jnp.broadcast_to(rhs[None], (groups,) + field), "tm", 0, 0, axis_index_groups=across)
    points, value, defect = call(
        correct_kernel,
        [(STEPS_DEV,) + pair, (1,) + pair, (1,) + pair],
        [FINE, MIDDLE, COARSE],
        rhs,
        shares,
        first,
        initial,
        feed_rate,
        kill_rate,
    )
    return points, residual[None], value, defect


def solution(mesh):
    in_specs = (P(), P("tm", None, None, None), P(), P())
    out_specs = (P("tm", None, None, None),) * 4
    return jax.shard_map(shards, mesh=mesh, in_specs=in_specs, out_specs=out_specs, check_vma=False)
```

```python
import functools

import jax
import jax.numpy as jnp
import ml_dtypes
import numpy as np
from jax import lax
from jax.experimental import pallas as pl
from jax.experimental.pallas import tpu as pltpu
from jax.sharding import PartitionSpec as P

GRID = 64
GROUP = 16
STEPS_DEV = 4
LANES = 2 * GRID
diffusion = (0.2, 0.1)
interval_time = 0.03125
fine_step = interval_time / STEPS_DEV
level_step = interval_time
coarse_step = interval_time * GROUP


def basis_tables():
    positions = np.arange(GRID, dtype=np.float32)
    angles = np.float32(np.pi) * (positions[:, None] + np.float32(0.5)) * positions[None] / np.float32(GRID)
    weight = np.where(positions == 0, np.sqrt(np.float32(1 / GRID)), np.sqrt(np.float32(2 / GRID)))
    cosines = np.cos(angles.astype(np.float64)).astype(np.float32)
    basis = cosines * weight[None].astype(np.float32)
    sines = np.sin((np.float32(np.pi) * positions / np.float32(2 * GRID)).astype(np.float64)).astype(np.float32)
    return basis.astype(np.float64), (np.float32(-4) * sines * sines).astype(np.float64)


def solve_terms(time_step, rate, rank):
    basis, values = basis_tables()
    inverse = 1 / (1 - time_step * rate * (values[:, None] + values[None]))
    side = inverse[:, 0] - 1
    rest = inverse - 1 - side[:, None] - side[None]
    weights, vectors = np.linalg.eigh(rest)
    order = np.argsort(-np.abs(weights))[:rank]
    first = (basis * side) @ basis.T + basis @ basis.T - np.eye(GRID)
    cross = [(basis * (vectors[:, k] * np.sqrt(np.abs(weights[k])))) @ basis.T for k in order]
    return first, cross, [np.sign(weights[k]) for k in order]


def halves(matrix):
    high = matrix.astype(np.float32).astype(ml_dtypes.bfloat16)
    low = (matrix - high.astype(np.float64)).astype(np.float32).astype(ml_dtypes.bfloat16)
    return high, low


def twice(matrix):
    return np.concatenate([matrix, matrix], 1)


def species_tables(time_step, rate, rank, fine_cross):
    first, cross, signs = solve_terms(time_step, rate, rank)
    high, low = halves(first)
    right = np.concatenate([twice(high), twice(high), twice(low), np.zeros_like(twice(low))], 0)
    left = [high, high, low]
    cross_high, cross_low = zip(*[halves(m) for m in cross])
    cross_high = np.concatenate([twice(m) for m in cross_high], 1)
    cross_low = np.concatenate([twice(m) for m in cross_low], 1)
    parts = [cross_high, cross_high, cross_low] if fine_cross else [cross_high, cross_low]
    blank = np.zeros((4 * GRID - GRID * len(parts), cross_high.shape[1]), ml_dtypes.bfloat16)
    mixing = np.concatenate(parts + [blank], 0)
    signed_high, signed_low = halves(np.concatenate([m * s for m, s in zip(cross, signs)], 1))
    left += [signed_high, signed_high, signed_low] if fine_cross else [signed_high]
    return right, mixing, np.concatenate(left, 1)


@functools.lru_cache(None)
def level_tables(time_step, rank, fine_cross):
    sub = species_tables(time_step, diffusion[0], rank, fine_cross)
    cat = species_tables(time_step, diffusion[1], rank, fine_cross)
    left = np.concatenate([sub[2], cat[2]], 0)
    left = np.concatenate([left, np.zeros_like(left)], 0)
    return np.concatenate([sub[0], cat[0], sub[1], cat[1], left], 1)


def product(left, right):
    return jnp.dot(left, right, preferred_element_type=jnp.float32)


def second_half():
    return lax.broadcasted_iota(jnp.int32, (GRID, LANES), 1) >= GRID


def spread(fields):
    turned = pltpu.roll(fields, GRID, 1)
    second = second_half()
    return jnp.where(second, turned, fields), jnp.where(second, fields, turned)


def merge(state):
    return jnp.where(second_half(), state[1], state[0])


def loaded(pair):
    return tuple(jnp.concatenate([pair[i], pair[i]], 1) for i in range(2))


def unpack_to(ref, state):
    ref[0] = state[0][:, :GRID]
    ref[1] = state[1][:, :GRID]


def choose(condition, one, other):
    return tuple(jnp.where(condition, a, b) for a, b in zip(one, other))


def plus(one, other):
    return tuple(a + b for a, b in zip(one, other))


def minus(one, other):
    return tuple(a - b for a, b in zip(one, other))


class Level:
    def __init__(self, time_step, rank, fine_cross):
        self.time_step, self.rank, self.fine_cross = time_step, rank, fine_cross
        self.tables = level_tables(time_step, rank, fine_cross)
        self.width = self.tables.shape[1]

    def bind(self, table, start, feed, kill):
        h = jnp.float32(self.time_step)
        rank, fine_cross = self.rank, self.fine_cross
        cross = LANES * rank
        second = second_half()
        supply, decay = h * feed, h * (feed + kill)
        right_at, cross_at = start, start + 2 * LANES
        left_at = cross_at + 2 * cross
        deep = slice(0, 4 * GRID if fine_cross else 2 * GRID)

        def solve(values):
            made = []
            for i, value in enumerate(values):
                high = value.astype(jnp.bfloat16)
                rest = value - high.astype(jnp.float32)
                mixed = jnp.where(second, rest, value).astype(jnp.bfloat16)
                wide = jnp.concatenate([mixed, high], 1)
                weights = table[deep, cross_at + cross * i : cross_at + cross * (i + 1)]
                made.append((high, rest, wide, product(wide if fine_cross else high, weights)))
            solved = []
            for i, (value, (high, rest, wide, turned)) in enumerate(zip(values, made)):
                right = product(wide, table[:, right_at + LANES * i : right_at + LANES * (i + 1)])
                turned = jnp.concatenate([turned[:, LANES * k : LANES * (k + 1)] for k in range(rank)], 0)
                turned_high = turned.astype(jnp.bfloat16)
                stack = [high, rest.astype(jnp.bfloat16), high, turned_high]
                if fine_cross:
                    stack += [(turned - turned_high.astype(jnp.float32)).astype(jnp.bfloat16), turned_high]
                stack = jnp.concatenate(stack, 0)
                left = table[GRID * i : GRID * (i + 1), left_at : left_at + stack.shape[0]]
                solved.append((right, product(left, stack)))
            return solved

        def step(state, extra=None):
            sub, cat = state
            uptake = h * (sub * cat * cat)
            values = (sub + (supply - supply * sub - uptake), cat + (uptake - decay * cat))
            sums = [a + b for a, b in solve(values)]
            if extra is not None:
                sums = [a + b for a, b in zip(sums, extra)]
            return tuple(a + b for a, b in zip(values, sums))

        return step


FINE = Level(fine_step, 1, False)
MIDDLE = Level(level_step, 1, True)
COARSE = Level(coarse_step, 3, True)
near_tables = np.concatenate([FINE.tables, MIDDLE.tables], 1)
far_tables = COARSE.tables


def fetch_kernel(near_in, far_in, initial_in, feed_in, kill_in, near_out, far_out, initial, feed, kill, sems):
    pairs = [(near_in, near_out), (far_in, far_out), (initial_in, initial), (feed_in, feed), (kill_in, kill)]
    copies = [pltpu.make_async_copy(a, b, sems.at[i]) for i, (a, b) in enumerate(pairs)]
    for copy in copies:
        copy.start()
    for copy in copies:
        copy.wait()


def relax_kernel(near_ref, far_ref, table, initial, feed, kill, share_ref, residual_ref):
    rates = [jnp.concatenate([r[...]] * 2, 1) for r in (feed, kill)]
    fine = FINE.bind(table, 0, *rates)
    middle = MIDDLE.bind(table, FINE.width, *rates)
    position = lax.axis_index("tm")
    first = loaded(initial)
    own = choose(position == 0, first, loaded(near_ref))
    prior = choose(position == 1, first, loaded(far_ref))
    for _ in range(STEPS_DEV):
        own, prior = fine(own), fine(prior)
    shifted = choose(position == 0, first, prior)
    leap = middle(shifted)
    arrived = shifted
    for _ in range(STEPS_DEV):
        arrived = fine(arrived)
    share_ref[...] = merge(choose(position % GROUP == 0, shifted, minus(arrived, leap)))
    unpack_to(residual_ref, minus(arrived, own))


def bound(near_table, far_table, feed_ref, kill_ref):
    rates = [jnp.concatenate([r[...]] * 2, 1) for r in (feed_ref, kill_ref)]
    return (
        FINE.bind(near_table, 0, *rates),
        MIDDLE.bind(near_table, FINE.width, *rates),
        COARSE.bind(far_table, 0, *rates),
    )


def chain(step, load, state, start, stop, block, keep=None):
    def turn(t, state):
        for i in range(block):
            j = start + t * block + i
            state = step(state, spread(load(j)))
            if keep is not None:
                keep[j + 1] = merge(state)
        return state

    return lax.fori_loop(0, (stop - start) // block, turn, state)


def group_kernel(shares_ref, near_table, far_table, feed_ref, kill_ref, first_ref, rhs_ref):
    fine, middle, coarse = bound(near_table, far_table, feed_ref, kill_ref)
    start = spread(shares_ref[0])
    state = start
    for _ in range(STEPS_DEV):
        state = fine(state)
    leap, handed = middle(start), coarse(start)
    first_ref[...] = merge(minus(state, leap))
    state = chain(middle, lambda j: shares_ref[j], state, 1, GROUP, 5)
    position = lax.axis_index("tm")
    rhs = merge(choose(position < GROUP, state, minus(state, handed)))
    rhs_ref[...] = jnp.where(position % 2 == 0, rhs[: GRID // 2], rhs[GRID // 2 :])


def correct_kernel(
    mine_ref, other_ref, shares_ref, first_ref, initial_ref, near_table, far_table, feed_ref, kill_ref,
    points_ref, value_ref, defect_ref, coarse_kept, middle_kept,
):
    fine, middle, coarse = bound(near_table, far_table, feed_ref, kill_ref)
    position = lax.axis_index("tm")
    member, group_id = position % GROUP, position // GROUP
    upper = position % 2 == 0

    def coarse_side(g):
        mine, other = mine_ref[g], other_ref[g]
        return jnp.concatenate([jnp.where(upper, mine, other), jnp.where(upper, other, mine)], 0)

    groups = mine_ref.shape[0]
    coarse_kept[0] = merge(loaded(initial_ref))
    coarse_kept[1] = coarse_side(0)
    state = coarse(spread(coarse_side(0)), spread(coarse_side(1)))
    coarse_kept[2] = merge(state)
    chain(coarse, coarse_side, state, 2, groups, 5, coarse_kept)
    earlier, value = spread(coarse_kept[group_id]), spread(coarse_kept[group_id + 1])
    unpack_to(value_ref.at[0], value)
    middle_kept[0] = merge(earlier)
    state = middle(earlier, spread(first_ref[...]))
    middle_kept[1] = merge(state)
    chain(middle, lambda j: shares_ref[j], state, 1, GROUP - 1, 7, middle_kept)
    prior = spread(middle_kept[member])
    side = spread(jnp.where(member == 0, first_ref[...], shares_ref[member]))
    updated = middle(prior, side)
    closing = member == GROUP - 1
    state = prior
    for i in range(STEPS_DEV - 1):
        state = fine(state)
        unpack_to(points_ref.at[i], state)
    unpack_to(points_ref.at[STEPS_DEV - 1], choose(closing, value, updated))
    unpack_to(defect_ref.at[0], choose(closing, minus(updated, value), minus(value, value)))


VMEM = pl.BlockSpec(memory_space=pltpu.VMEM)
ANY = pl.BlockSpec(memory_space=pl.ANY)


def call(kernel, outs, in_specs, scratch, limit, *operands, cost=None):
    return pl.pallas_call(
        kernel,
        out_shape=[o if isinstance(o, jax.ShapeDtypeStruct) else jax.ShapeDtypeStruct(o, jnp.float32) for o in outs],
        in_specs=in_specs,
        out_specs=[VMEM] * len(outs),
        scratch_shapes=scratch,
        cost_estimate=cost,
        compiler_params=pltpu.CompilerParams(vmem_limit_bytes=limit * 2**20),
    )(*operands)


def shards(initial, coarse_guess, feed_rate, kill_rate):
    devices = lax.axis_size("tm")
    groups = devices // GROUP
    field, pair, half, plane = (GRID, LANES), (2, GRID, GRID), (GRID // 2, LANES), (GRID, GRID)
    own = coarse_guess[0]
    near = lax.ppermute(own, "tm", [(i, i + 1) for i in range(devices - 1)])
    far = lax.ppermute(own, "tm", [(i, i + 2) for i in range(devices - 2)])
    near_table, far_table, initial, feed_rate, kill_rate = call(
        fetch_kernel,
        [jax.ShapeDtypeStruct(t.shape, jnp.bfloat16) for t in (near_tables, far_tables)] + [pair, plane, plane],
        [ANY] * 5,
        [pltpu.SemaphoreType.DMA((5,))],
        16,
        jnp.asarray(near_tables), jnp.asarray(far_tables), initial, feed_rate, kill_rate,
        cost=pl.CostEstimate(flops=0, bytes_accessed=4 * near_tables.size + 4 * far_tables.size, transcendentals=0),
    )
    share, residual = call(
        relax_kernel, [field, pair], [VMEM] * 6, [], 16, near, far, near_table, initial, feed_rate, kill_rate
    )
    inside = [[g * GROUP + m for m in range(GROUP)] for g in range(groups)]
    shares = lax.all_gather(share, "tm", axis_index_groups=inside)
    first, rhs = call(
        group_kernel, [field, half], [VMEM] * 5, [], 16, shares, near_table, far_table, feed_rate, kill_rate
    )
    across = [[g * GROUP + m for g in range(groups)] for m in range(GROUP)]
    mine = lax.all_to_all(jnp.broadcast_to(rhs[None], (groups,) + half), "tm", 0, 0, axis_index_groups=across)
    other = lax.ppermute(mine, "tm", [(i, i ^ 1) for i in range(devices)])
    points, value, defect = call(
        correct_kernel,
        [(STEPS_DEV,) + pair, (1,) + pair, (1,) + pair],
        [VMEM] * 9,
        [pltpu.VMEM((groups + 1,) + field, jnp.float32), pltpu.VMEM((GROUP,) + field, jnp.float32)],
        16,
        mine, other, shares, first, initial, near_table, far_table, feed_rate, kill_rate,
    )
    return points, residual[None], value, defect


def solution(mesh):
    in_specs = (P(), P("tm", None, None, None), P(), P())
    out_specs = (P("tm", None, None, None),) * 4
    return jax.shard_map(shards, mesh=mesh, in_specs=in_specs, out_specs=out_specs, check_vma=False)
```

```python
import functools

import jax
import jax.numpy as jnp
import ml_dtypes
import numpy as np
from jax import lax
from jax.experimental import pallas as pl
from jax.experimental.pallas import tpu as pltpu
from jax.sharding import PartitionSpec as P

GRID = 64
GROUP = 16
STEPS_DEV = 4
LANES = 2 * GRID
diffusion = (0.2, 0.1)
interval_time = 0.03125
fine_step = interval_time / STEPS_DEV
level_step = interval_time
coarse_step = interval_time * GROUP


def basis_tables():
    positions = np.arange(GRID, dtype=np.float32)
    angles = np.float32(np.pi) * (positions[:, None] + np.float32(0.5)) * positions[None] / np.float32(GRID)
    weight = np.where(positions == 0, np.sqrt(np.float32(1 / GRID)), np.sqrt(np.float32(2 / GRID)))
    cosines = np.cos(angles.astype(np.float64)).astype(np.float32)
    basis = cosines * weight[None].astype(np.float32)
    sines = np.sin((np.float32(np.pi) * positions / np.float32(2 * GRID)).astype(np.float64)).astype(np.float32)
    return basis.astype(np.float64), (np.float32(-4) * sines * sines).astype(np.float64)


def solve_terms(time_step, rate, rank):
    basis, values = basis_tables()
    inverse = 1 / (1 - time_step * rate * (values[:, None] + values[None]))
    side = inverse[:, 0] - 1
    rest = inverse - 1 - side[:, None] - side[None]
    weights, vectors = np.linalg.eigh(rest)
    order = np.argsort(-np.abs(weights))[:rank]
    first = (basis * side) @ basis.T + basis @ basis.T - np.eye(GRID)
    cross = [(basis * (vectors[:, k] * np.sqrt(np.abs(weights[k])))) @ basis.T for k in order]
    return first, cross, [np.sign(weights[k]) for k in order]


def halves(matrix):
    high = matrix.astype(np.float32).astype(ml_dtypes.bfloat16)
    low = (matrix - high.astype(np.float64)).astype(np.float32).astype(ml_dtypes.bfloat16)
    return high, low


def twice(matrix):
    return np.concatenate([matrix, matrix], 1)


def species_tables(time_step, rate, rank, fine_cross):
    first, cross, signs = solve_terms(time_step, rate, rank)
    high, low = halves(first)
    right = np.concatenate([twice(high), twice(high), twice(low), np.zeros_like(twice(low))], 0)
    left = [high, high, low]
    cross_high, cross_low = zip(*[halves(m) for m in cross])
    cross_high = np.concatenate([twice(m) for m in cross_high], 1)
    cross_low = np.concatenate([twice(m) for m in cross_low], 1)
    parts = [cross_high, cross_high, cross_low] if fine_cross else [cross_high, cross_low]
    blank = np.zeros((4 * GRID - GRID * len(parts), cross_high.shape[1]), ml_dtypes.bfloat16)
    mixing = np.concatenate(parts + [blank], 0)
    for k, (matrix, sign) in enumerate(zip(cross, signs)):
        high, low = halves(matrix * sign)
        left += [high, high, low] if k < fine_cross else [high]
    return right, mixing, np.concatenate(left, 1)


@functools.lru_cache(None)
def level_tables(time_step, rank, fine_cross):
    sub = species_tables(time_step, diffusion[0], rank, fine_cross)
    cat = species_tables(time_step, diffusion[1], rank, fine_cross)
    left = np.concatenate([sub[2], cat[2]], 0)
    left = np.concatenate([left, np.zeros_like(left)], 0)
    return np.concatenate([sub[0], cat[0], sub[1], cat[1], left], 1)


def product(left, right):
    return jnp.dot(left, right, preferred_element_type=jnp.float32)


def second_half():
    return lax.broadcasted_iota(jnp.int32, (GRID, LANES), 1) >= GRID


def spread(fields):
    turned = pltpu.roll(fields, GRID, 1)
    second = second_half()
    return jnp.where(second, turned, fields), jnp.where(second, fields, turned)


def merge(state):
    return jnp.where(second_half(), state[1], state[0])


def loaded(pair):
    return tuple(jnp.concatenate([pair[i], pair[i]], 1) for i in range(2))


def unpack_to(ref, state):
    ref[0] = state[0][:, :GRID]
    ref[1] = state[1][:, :GRID]


def choose(condition, one, other):
    return tuple(jnp.where(condition, a, b) for a, b in zip(one, other))


def plus(one, other):
    return tuple(a + b for a, b in zip(one, other))


def minus(one, other):
    return tuple(a - b for a, b in zip(one, other))


class Level:
    def __init__(self, time_step, rank, fine_cross):
        self.time_step, self.rank, self.fine_cross = time_step, rank, fine_cross
        self.tables = level_tables(time_step, rank, fine_cross)
        self.width = self.tables.shape[1]

    def bind(self, table, start, feed, kill):
        h = jnp.float32(self.time_step)
        rank, fine_cross = self.rank, self.fine_cross
        cross = LANES * rank
        second = second_half()
        supply, decay = h * feed, h * (feed + kill)
        right_at, cross_at = start, start + 2 * LANES
        left_at = cross_at + 2 * cross
        deep = slice(0, 4 * GRID if fine_cross else 2 * GRID)

        def solve(values):
            made = []
            for i, value in enumerate(values):
                high = value.astype(jnp.bfloat16)
                rest = value - high.astype(jnp.float32)
                mixed = jnp.where(second, rest, value).astype(jnp.bfloat16)
                wide = jnp.concatenate([mixed, high], 1)
                weights = table[deep, cross_at + cross * i : cross_at + cross * (i + 1)]
                made.append((high, rest, wide, product(wide if fine_cross else high, weights)))
            solved = []
            for i, (value, (high, rest, wide, turned)) in enumerate(zip(values, made)):
                right = product(wide, table[:, right_at + LANES * i : right_at + LANES * (i + 1)])
                stack = [high, rest.astype(jnp.bfloat16), high]
                for k in range(rank):
                    part = turned[:, LANES * k : LANES * (k + 1)]
                    part_high = part.astype(jnp.bfloat16)
                    stack.append(part_high)
                    if k < fine_cross:
                        stack += [(part - part_high.astype(jnp.float32)).astype(jnp.bfloat16), part_high]
                stack = jnp.concatenate(stack, 0)
                left = table[GRID * i : GRID * (i + 1), left_at : left_at + stack.shape[0]]
                solved.append((right, product(left, stack)))
            return solved

        def step(state, extra=None):
            sub, cat = state
            uptake = h * (sub * cat * cat)
            values = (sub + (supply - supply * sub - uptake), cat + (uptake - decay * cat))
            sums = [a + b for a, b in solve(values)]
            if extra is not None:
                sums = [a + b for a, b in zip(sums, extra)]
            return tuple(a + b for a, b in zip(values, sums))

        return step


FINE = Level(fine_step, 1, 0)
MIDDLE = Level(level_step, 1, 1)
COARSE = Level(coarse_step, 3, 1)
near_tables = np.concatenate([FINE.tables, MIDDLE.tables], 1)
far_tables = COARSE.tables


def fetch_kernel(near_in, far_in, initial_in, feed_in, kill_in, near_out, far_out, initial, feed, kill, sems):
    pairs = [(near_in, near_out), (far_in, far_out), (initial_in, initial), (feed_in, feed), (kill_in, kill)]
    copies = [pltpu.make_async_copy(a, b, sems.at[i]) for i, (a, b) in enumerate(pairs)]
    for copy in copies:
        copy.start()
    for copy in copies:
        copy.wait()


def relax_kernel(near_ref, far_ref, table, initial, feed, kill, share_ref, residual_ref):
    rates = [jnp.concatenate([r[...]] * 2, 1) for r in (feed, kill)]
    fine = FINE.bind(table, 0, *rates)
    middle = MIDDLE.bind(table, FINE.width, *rates)
    position = lax.axis_index("tm")
    first = loaded(initial)
    own = choose(position == 0, first, loaded(near_ref))
    prior = choose(position == 1, first, loaded(far_ref))
    for _ in range(STEPS_DEV):
        own, prior = fine(own), fine(prior)
    shifted = choose(position == 0, first, prior)
    leap = middle(shifted)
    arrived = shifted
    for _ in range(STEPS_DEV):
        arrived = fine(arrived)
    share_ref[...] = merge(choose(position % GROUP == 0, shifted, minus(arrived, leap)))
    unpack_to(residual_ref, minus(arrived, own))


def bound(near_table, far_table, feed_ref, kill_ref):
    rates = [jnp.concatenate([r[...]] * 2, 1) for r in (feed_ref, kill_ref)]
    return (
        FINE.bind(near_table, 0, *rates),
        MIDDLE.bind(near_table, FINE.width, *rates),
        COARSE.bind(far_table, 0, *rates),
    )


def chain(step, load, state, start, stop, block, keep=None):
    def turn(t, state):
        for i in range(block):
            j = start + t * block + i
            state = step(state, spread(load(j)))
            if keep is not None:
                keep[j + 1] = merge(state)
        return state

    return lax.fori_loop(0, (stop - start) // block, turn, state)


def group_kernel(shares_ref, near_table, far_table, feed_ref, kill_ref, first_ref, rhs_ref, half_ref):
    fine, middle, coarse = bound(near_table, far_table, feed_ref, kill_ref)
    start = spread(shares_ref[0])
    state = start
    for _ in range(STEPS_DEV):
        state = fine(state)
    leap, handed = middle(start), coarse(start)
    first_ref[...] = merge(minus(state, leap))
    state = chain(middle, lambda j: shares_ref[j], state, 1, GROUP, 5)
    position = lax.axis_index("tm")
    rhs = merge(choose(position < GROUP, state, minus(state, handed)))
    rhs_ref[...] = rhs
    half_ref[...] = jnp.where(position % 2 == 0, rhs[: GRID // 2], rhs[GRID // 2 :])


def correct_kernel(
    sides_ref, rhs_ref, shares_ref, first_ref, initial_ref, near_table, far_table, feed_ref, kill_ref,
    points_ref, value_ref, defect_ref, coarse_kept, middle_kept,
):
    fine, middle, coarse = bound(near_table, far_table, feed_ref, kill_ref)
    position = lax.axis_index("tm")
    member, group_id = position % GROUP, position // GROUP

    def coarse_side(g):
        return jnp.concatenate([sides_ref[0, g], sides_ref[1, g]], 0)

    coarse_kept[0] = merge(loaded(initial_ref))
    coarse_kept[1] = coarse_side(0)
    chain(coarse, coarse_side, spread(coarse_side(0)), 1, sides_ref.shape[1], 5, coarse_kept)
    earlier = spread(coarse_kept[group_id])
    own_side = spread(rhs_ref[...])
    value = choose(group_id == 0, own_side, coarse(earlier, own_side))
    unpack_to(value_ref.at[0], value)
    middle_kept[0] = merge(earlier)
    state = middle(earlier, spread(first_ref[...]))
    middle_kept[1] = merge(state)
    chain(middle, lambda j: shares_ref[j], state, 1, GROUP - 1, 7, middle_kept)
    prior = spread(middle_kept[member])
    side = spread(jnp.where(member == 0, first_ref[...], shares_ref[member]))
    updated = middle(prior, side)
    closing = member == GROUP - 1
    state = prior
    for i in range(STEPS_DEV - 1):
        state = fine(state)
        unpack_to(points_ref.at[i], state)
    unpack_to(points_ref.at[STEPS_DEV - 1], choose(closing, value, updated))
    unpack_to(defect_ref.at[0], choose(closing, minus(updated, value), minus(value, value)))


VMEM = pl.BlockSpec(memory_space=pltpu.VMEM)
HBM = pl.BlockSpec(memory_space=pltpu.HBM)


def call(kernel, outs, in_specs, scratch, limit, *operands, cost=None):
    return pl.pallas_call(
        kernel,
        out_shape=[o if isinstance(o, jax.ShapeDtypeStruct) else jax.ShapeDtypeStruct(o, jnp.float32) for o in outs],
        in_specs=in_specs,
        out_specs=[VMEM] * len(outs),
        scratch_shapes=scratch,
        cost_estimate=cost,
        compiler_params=pltpu.CompilerParams(vmem_limit_bytes=limit * 2**20),
    )(*operands)


def shards(initial, coarse_guess, feed_rate, kill_rate):
    devices = lax.axis_size("tm")
    groups = devices // GROUP
    field, pair, half, plane = (GRID, LANES), (2, GRID, GRID), (GRID // 2, LANES), (GRID, GRID)
    own = coarse_guess[0]
    near = lax.ppermute(own, "tm", [(i, i + 1) for i in range(devices - 1)])
    far = lax.ppermute(own, "tm", [(i, i + 2) for i in range(devices - 2)])
    near_table, far_table, initial, feed_rate, kill_rate = call(
        fetch_kernel,
        [jax.ShapeDtypeStruct(t.shape, jnp.bfloat16) for t in (near_tables, far_tables)] + [pair, plane, plane],
        [HBM] * 5,
        [pltpu.SemaphoreType.DMA((5,))],
        16,
        jnp.asarray(near_tables), jnp.asarray(far_tables), initial, feed_rate, kill_rate,
        cost=pl.CostEstimate(flops=0, bytes_accessed=4 * near_tables.size + 4 * far_tables.size, transcendentals=0),
    )
    share, residual = call(
        relax_kernel, [field, pair], [VMEM] * 6, [], 16, near, far, near_table, initial, feed_rate, kill_rate
    )
    inside = [[g * GROUP + m for m in range(GROUP)] for g in range(groups)]
    shares = lax.all_gather(share, "tm", axis_index_groups=inside)
    first, rhs, part = call(
        group_kernel, [field, field, half], [VMEM] * 5, [], 16, shares, near_table, far_table, feed_rate, kill_rate
    )
    across = [[g * GROUP + m for g in range(groups)] for m in range(GROUP)]
    parts = lax.all_to_all(jnp.broadcast_to(part[None], (groups,) + half), "tm", 0, 0, axis_index_groups=across)
    cores = [[2 * c, 2 * c + 1] for c in range(devices // 2)]
    sides = lax.all_gather(parts[: groups - 1], "tm", axis_index_groups=cores)
    points, value, defect = call(
        correct_kernel,
        [(STEPS_DEV,) + pair, (1,) + pair, (1,) + pair],
        [VMEM] * 9,
        [pltpu.VMEM((groups,) + field, jnp.float32), pltpu.VMEM((GROUP,) + field, jnp.float32)],
        16,
        sides, rhs, shares, first, initial, near_table, far_table, feed_rate, kill_rate,
    )
    return points, residual[None], value, defect


def solution(mesh):
    in_specs = (P(), P("tm", None, None, None), P(), P())
    out_specs = (P("tm", None, None, None),) * 4
    return jax.shard_map(shards, mesh=mesh, in_specs=in_specs, out_specs=out_specs, check_vma=False)
```

```python
import functools

import jax
import jax.numpy as jnp
import ml_dtypes
import numpy as np
from jax import lax
from jax.experimental import pallas as pl
from jax.experimental.pallas import tpu as pltpu
from jax.sharding import PartitionSpec as P

GRID = 64
GROUP = 16
STEPS_DEV = 4
LANES = 2 * GRID
diffusion = (0.2, 0.1)
interval_time = 0.03125
fine_step = interval_time / STEPS_DEV
level_step = interval_time
coarse_step = interval_time * GROUP


def basis_tables():
    positions = np.arange(GRID, dtype=np.float32)
    angles = np.float32(np.pi) * (positions[:, None] + np.float32(0.5)) * positions[None] / np.float32(GRID)
    weight = np.where(positions == 0, np.sqrt(np.float32(1 / GRID)), np.sqrt(np.float32(2 / GRID)))
    cosines = np.cos(angles.astype(np.float64)).astype(np.float32)
    basis = cosines * weight[None].astype(np.float32)
    sines = np.sin((np.float32(np.pi) * positions / np.float32(2 * GRID)).astype(np.float64)).astype(np.float32)
    return basis.astype(np.float64), (np.float32(-4) * sines * sines).astype(np.float64)


def solve_terms(time_step, rate, rank):
    basis, values = basis_tables()
    inverse = 1 / (1 - time_step * rate * (values[:, None] + values[None]))
    side = inverse[:, 0] - 1
    rest = inverse - 1 - side[:, None] - side[None]
    weights, vectors = np.linalg.eigh(rest)
    order = np.argsort(-np.abs(weights))[:rank]
    first = (basis * side) @ basis.T + basis @ basis.T - np.eye(GRID)
    cross = [(basis * (vectors[:, k] * np.sqrt(np.abs(weights[k])))) @ basis.T for k in order]
    return first, cross, [np.sign(weights[k]) for k in order]


def halves(matrix):
    high = matrix.astype(np.float32).astype(ml_dtypes.bfloat16)
    low = (matrix - high.astype(np.float64)).astype(np.float32).astype(ml_dtypes.bfloat16)
    return high, low


def twice(matrix):
    return np.concatenate([matrix, matrix], 1)


def species_tables(time_step, rate, rank, fine_cross):
    first, cross, signs = solve_terms(time_step, rate, rank)
    high, low = halves(first)
    right = np.concatenate([twice(high), twice(high), twice(low), np.zeros_like(twice(low))], 0)
    left = [high, high, low]
    cross_high, cross_low = zip(*[halves(m) for m in cross])
    cross_high = np.concatenate([twice(m) for m in cross_high], 1)
    cross_low = np.concatenate([twice(m) for m in cross_low], 1)
    parts = [cross_high, cross_high, cross_low] if fine_cross else [cross_high, cross_low]
    blank = np.zeros((4 * GRID - GRID * len(parts), cross_high.shape[1]), ml_dtypes.bfloat16)
    mixing = np.concatenate(parts + [blank], 0)
    for k, (matrix, sign) in enumerate(zip(cross, signs)):
        high, low = halves(matrix * sign)
        left += [high, high, low] if k < fine_cross else [high]
    return right, mixing, np.concatenate(left, 1)


@functools.lru_cache(None)
def level_tables(time_step, rank, fine_cross):
    sub = species_tables(time_step, diffusion[0], rank, fine_cross)
    cat = species_tables(time_step, diffusion[1], rank, fine_cross)
    left = np.concatenate([sub[2], cat[2]], 0)
    left = np.concatenate([left, np.zeros_like(left)], 0)
    return np.concatenate([sub[0], cat[0], sub[1], cat[1], left], 1)


def product(left, right):
    return jnp.dot(left, right, preferred_element_type=jnp.float32)


def second_half():
    return lax.broadcasted_iota(jnp.int32, (GRID, LANES), 1) >= GRID


def spread(fields):
    turned = pltpu.roll(fields, GRID, 1)
    second = second_half()
    return jnp.where(second, turned, fields), jnp.where(second, fields, turned)


def merge(state):
    return jnp.where(second_half(), state[1], state[0])


def loaded(pair):
    return tuple(jnp.concatenate([pair[i], pair[i]], 1) for i in range(2))


def unpack_to(ref, state):
    ref[0] = state[0][:, :GRID]
    ref[1] = state[1][:, :GRID]


def choose(condition, one, other):
    return tuple(jnp.where(condition, a, b) for a, b in zip(one, other))


def plus(one, other):
    return tuple(a + b for a, b in zip(one, other))


def minus(one, other):
    return tuple(a - b for a, b in zip(one, other))


class Level:
    def __init__(self, time_step, rank, fine_cross):
        self.time_step, self.rank, self.fine_cross = time_step, rank, fine_cross
        self.tables = level_tables(time_step, rank, fine_cross)
        self.width = self.tables.shape[1]

    def bind(self, table, start, feed, kill):
        h = jnp.float32(self.time_step)
        rank, fine_cross = self.rank, self.fine_cross
        cross = LANES * rank
        second = second_half()
        supply, decay = h * feed, h * (feed + kill)
        right_at, cross_at = start, start + 2 * LANES
        left_at = cross_at + 2 * cross
        deep = slice(0, 4 * GRID if fine_cross else 2 * GRID)

        def solve(values):
            made = []
            for i, value in enumerate(values):
                high = value.astype(jnp.bfloat16)
                rest = value - high.astype(jnp.float32)
                mixed = jnp.where(second, rest, value).astype(jnp.bfloat16)
                wide = jnp.concatenate([mixed, high], 1)
                weights = table[deep, cross_at + cross * i : cross_at + cross * (i + 1)]
                made.append((high, rest, wide, product(wide if fine_cross else high, weights)))
            solved = []
            for i, (value, (high, rest, wide, turned)) in enumerate(zip(values, made)):
                right = product(wide, table[:, right_at + LANES * i : right_at + LANES * (i + 1)])
                stack = [high, rest.astype(jnp.bfloat16), high]
                for k in range(rank):
                    part = turned[:, LANES * k : LANES * (k + 1)]
                    part_high = part.astype(jnp.bfloat16)
                    stack.append(part_high)
                    if k < fine_cross:
                        stack += [(part - part_high.astype(jnp.float32)).astype(jnp.bfloat16), part_high]
                stack = jnp.concatenate(stack, 0)
                left = table[GRID * i : GRID * (i + 1), left_at : left_at + stack.shape[0]]
                solved.append((right, product(left, stack)))
            return solved

        def step(state, extra=None):
            sub, cat = state
            uptake = h * (sub * cat * cat)
            values = (sub + (supply - supply * sub - uptake), cat + (uptake - decay * cat))
            sums = [a + b for a, b in solve(values)]
            if extra is not None:
                sums = [a + b for a, b in zip(sums, extra)]
            return tuple(a + b for a, b in zip(values, sums))

        return step


FINE = Level(fine_step, 1, 0)
MIDDLE = Level(level_step, 1, 1)
COARSE = Level(coarse_step, 3, 1)
near_tables = np.concatenate([FINE.tables, MIDDLE.tables], 1)


def bound(fields, near_table, far_table=None):
    rates = loaded(fields.at[2:])
    fine, middle = FINE.bind(near_table, 0, *rates), MIDDLE.bind(near_table, FINE.width, *rates)
    return fine, middle, None if far_table is None else COARSE.bind(far_table, 0, *rates)


def relax_kernel(near_ref, far_ref, fields, near_table, share_ref, residual_ref):
    fine, middle, _ = bound(fields, near_table)
    position = lax.axis_index("tm")
    first = loaded(fields)
    own = choose(position == 0, first, loaded(near_ref))
    prior = choose(position == 1, first, loaded(far_ref))
    for _ in range(STEPS_DEV):
        own, prior = fine(own), fine(prior)
    shifted = choose(position == 0, first, prior)
    leap = middle(shifted)
    arrived = shifted
    for _ in range(STEPS_DEV):
        arrived = fine(arrived)
    share_ref[...] = merge(choose(position % GROUP == 0, shifted, minus(arrived, leap)))
    unpack_to(residual_ref, minus(arrived, own))


def chain(step, load, state, start, stop, block, keep=None):
    def turn(t, state):
        for i in range(block):
            j = start + t * block + i
            state = step(state, spread(load(j)))
            if keep is not None:
                keep[j + 1] = merge(state)
        return state

    return lax.fori_loop(0, (stop - start) // block, turn, state)


def group_kernel(shares_ref, fields, near_table, far_table, first_ref, rhs_ref, half_ref):
    fine, middle, coarse = bound(fields, near_table, far_table)
    start = spread(shares_ref[0])
    state = start
    for _ in range(STEPS_DEV):
        state = fine(state)
    leap, handed = middle(start), coarse(start)
    first_ref[...] = merge(minus(state, leap))
    state = chain(middle, lambda j: shares_ref[j], state, 1, GROUP, 5)
    position = lax.axis_index("tm")
    rhs = merge(choose(position < GROUP, state, minus(state, handed)))
    rhs_ref[...] = rhs
    half_ref[...] = jnp.where(position % 2 == 0, rhs[: GRID // 2], rhs[GRID // 2 :])


def correct_kernel(
    sides_ref, rhs_ref, shares_ref, first_ref, fields, near_table, far_table,
    points_ref, value_ref, defect_ref, coarse_kept, middle_kept,
):
    fine, middle, coarse = bound(fields, near_table, far_table)
    position = lax.axis_index("tm")
    member, group_id = position % GROUP, position // GROUP

    def coarse_side(g):
        return jnp.concatenate([sides_ref[0, g], sides_ref[1, g]], 0)

    coarse_kept[0] = merge(loaded(fields))
    coarse_kept[1] = coarse_side(0)
    chain(coarse, coarse_side, spread(coarse_side(0)), 1, sides_ref.shape[1], 5, coarse_kept)
    earlier = spread(coarse_kept[group_id])
    own_side = spread(rhs_ref[...])
    value = choose(group_id == 0, own_side, coarse(earlier, own_side))
    unpack_to(value_ref.at[0], value)
    middle_kept[0] = merge(earlier)
    state = middle(earlier, spread(first_ref[...]))
    middle_kept[1] = merge(state)
    chain(middle, lambda j: shares_ref[j], state, 1, GROUP - 1, 7, middle_kept)
    prior = spread(middle_kept[member])
    side = spread(jnp.where(member == 0, first_ref[...], shares_ref[member]))
    updated = middle(prior, side)
    closing = member == GROUP - 1
    state = prior
    for i in range(STEPS_DEV - 1):
        state = fine(state)
        unpack_to(points_ref.at[i], state)
    unpack_to(points_ref.at[STEPS_DEV - 1], choose(closing, value, updated))
    unpack_to(defect_ref.at[0], choose(closing, minus(updated, value), minus(value, value)))


VMEM = pl.BlockSpec(memory_space=pltpu.VMEM)


def call(kernel, outs, in_specs, scratch, limit, *operands):
    return pl.pallas_call(
        kernel,
        out_shape=[jax.ShapeDtypeStruct(o, jnp.float32) for o in outs],
        in_specs=in_specs,
        out_specs=[VMEM] * len(outs),
        scratch_shapes=scratch,
        compiler_params=pltpu.CompilerParams(vmem_limit_bytes=limit * 2**20),
    )(*operands)


def shards(initial, coarse_guess, feed_rate, kill_rate):
    devices = lax.axis_size("tm")
    groups = devices // GROUP
    field, pair, half = (GRID, LANES), (2, GRID, GRID), (GRID // 2, LANES)
    own = coarse_guess[0]
    near = lax.ppermute(own, "tm", [(i, i + 1) for i in range(devices - 1)])
    far = lax.ppermute(own, "tm", [(i, i + 2) for i in range(devices - 2)])
    near_table, far_table = jnp.asarray(near_tables), jnp.asarray(COARSE.tables)
    fields = jnp.concatenate([initial, feed_rate[None], kill_rate[None]], 0)
    share, residual = call(relax_kernel, [field, pair], [VMEM] * 4, [], 16, near, far, fields, near_table)
    inside = [[g * GROUP + m for m in range(GROUP)] for g in range(groups)]
    shares = lax.all_gather(share, "tm", axis_index_groups=inside)
    first, rhs, part = call(
        group_kernel, [field, field, half], [VMEM] * 4, [], 16, shares, fields, near_table, far_table
    )
    across = [[g * GROUP + m for g in range(groups)] for m in range(GROUP)]
    parts = lax.all_to_all(jnp.broadcast_to(part[None], (groups,) + half), "tm", 0, 0, axis_index_groups=across)
    cores = [[2 * c, 2 * c + 1] for c in range(devices // 2)]
    sides = lax.all_gather(parts[: groups - 1], "tm", axis_index_groups=cores)
    points, value, defect = call(
        correct_kernel,
        [(STEPS_DEV,) + pair, (1,) + pair, (1,) + pair],
        [VMEM] * 7,
        [pltpu.VMEM((groups,) + field, jnp.float32), pltpu.VMEM((GROUP,) + field, jnp.float32)],
        16,
        sides, rhs, shares, first, fields, near_table, far_table,
    )
    return points, residual[None], value, defect


def solution(mesh):
    in_specs = (P(), P("tm", None, None, None), P(), P())
    out_specs = (P("tm", None, None, None),) * 4
    return jax.shard_map(shards, mesh=mesh, in_specs=in_specs, out_specs=out_specs, check_vma=False)
```

```python
import functools

import jax
import jax.numpy as jnp
import ml_dtypes
import numpy as np
from jax import lax
from jax.experimental import pallas as pl
from jax.experimental.pallas import tpu as pltpu
from jax.sharding import PartitionSpec as P

GRID = 64
GROUP = 16
STEPS_DEV = 4
LANES = 2 * GRID
diffusion = (0.2, 0.1)
interval_time = 0.03125
fine_step = interval_time / STEPS_DEV
level_step = interval_time
coarse_step = interval_time * GROUP


def basis_tables():
    positions = np.arange(GRID, dtype=np.float32)
    angles = np.float32(np.pi) * (positions[:, None] + np.float32(0.5)) * positions[None] / np.float32(GRID)
    weight = np.where(positions == 0, np.sqrt(np.float32(1 / GRID)), np.sqrt(np.float32(2 / GRID)))
    cosines = np.cos(angles.astype(np.float64)).astype(np.float32)
    basis = cosines * weight[None].astype(np.float32)
    sines = np.sin((np.float32(np.pi) * positions / np.float32(2 * GRID)).astype(np.float64)).astype(np.float32)
    return basis.astype(np.float64), (np.float32(-4) * sines * sines).astype(np.float64)


def solve_terms(time_step, rate, rank):
    basis, values = basis_tables()
    inverse = 1 / (1 - time_step * rate * (values[:, None] + values[None]))
    side = inverse[:, 0] - 1
    rest = inverse - 1 - side[:, None] - side[None]
    weights, vectors = np.linalg.eigh(rest)
    order = np.argsort(-np.abs(weights))[:rank]
    first = (basis * side) @ basis.T + basis @ basis.T - np.eye(GRID)
    cross = [(basis * (vectors[:, k] * np.sqrt(np.abs(weights[k])))) @ basis.T for k in order]
    return first, cross, [np.sign(weights[k]) for k in order]


def halves(matrix):
    high = matrix.astype(np.float32).astype(ml_dtypes.bfloat16)
    low = (matrix - high.astype(np.float64)).astype(np.float32).astype(ml_dtypes.bfloat16)
    return high, low


def twice(matrix):
    return np.concatenate([matrix, matrix], 1)


def species_tables(time_step, rate, rank, fine_cross):
    first, cross, signs = solve_terms(time_step, rate, rank)
    high, low = halves(first)
    right = np.concatenate([twice(high), twice(high), twice(low), np.zeros_like(twice(low))], 0)
    left = [high, high, low]
    cross_high, cross_low = zip(*[halves(m) for m in cross])
    cross_high = np.concatenate([twice(m) for m in cross_high], 1)
    cross_low = np.concatenate([twice(m) for m in cross_low], 1)
    parts = [cross_high, cross_high, cross_low] if fine_cross else [cross_high, cross_low]
    blank = np.zeros((4 * GRID - GRID * len(parts), cross_high.shape[1]), ml_dtypes.bfloat16)
    mixing = np.concatenate(parts + [blank], 0)
    for k, (matrix, sign) in enumerate(zip(cross, signs)):
        high, low = halves(matrix * sign)
        left += [high, high, low] if k < fine_cross else [high]
    return right, mixing, np.concatenate(left, 1)


@functools.lru_cache(None)
def level_tables(time_step, rank, fine_cross):
    sub = species_tables(time_step, diffusion[0], rank, fine_cross)
    cat = species_tables(time_step, diffusion[1], rank, fine_cross)
    left = np.concatenate([sub[2], cat[2]], 0)
    left = np.concatenate([left, np.zeros_like(left)], 0)
    return np.concatenate([sub[0], cat[0], sub[1], cat[1], left], 1)


def product(left, right):
    return jnp.dot(left, right, preferred_element_type=jnp.float32)


def second_half():
    return lax.broadcasted_iota(jnp.int32, (GRID, LANES), 1) >= GRID


def spread(fields):
    turned = pltpu.roll(fields, GRID, 1)
    second = second_half()
    return jnp.where(second, turned, fields), jnp.where(second, fields, turned)


def merge(state):
    return jnp.where(second_half(), state[1], state[0])


def loaded(pair):
    return tuple(jnp.concatenate([pair[i], pair[i]], 1) for i in range(2))


def unpack_to(ref, state):
    ref[0] = state[0][:, :GRID]
    ref[1] = state[1][:, :GRID]


def choose(condition, one, other):
    return tuple(jnp.where(condition, a, b) for a, b in zip(one, other))


def plus(one, other):
    return tuple(a + b for a, b in zip(one, other))


def minus(one, other):
    return tuple(a - b for a, b in zip(one, other))


class Level:
    def __init__(self, time_step, rank, fine_cross):
        self.time_step, self.rank, self.fine_cross = time_step, rank, fine_cross
        self.tables = level_tables(time_step, rank, fine_cross)
        self.width = self.tables.shape[1]

    def bind(self, table, start, feed, kill):
        h = jnp.float32(self.time_step)
        rank, fine_cross = self.rank, self.fine_cross
        cross = LANES * rank
        second = second_half()
        supply, decay = h * feed, h * (feed + kill)
        right_at, cross_at = start, start + 2 * LANES
        left_at = cross_at + 2 * cross
        deep = slice(0, 4 * GRID if fine_cross else 2 * GRID)

        def solve(values):
            made = []
            for i, value in enumerate(values):
                high = value.astype(jnp.bfloat16)
                rest = value - high.astype(jnp.float32)
                mixed = jnp.where(second, rest, value).astype(jnp.bfloat16)
                wide = jnp.concatenate([mixed, high], 1)
                weights = table[deep, cross_at + cross * i : cross_at + cross * (i + 1)]
                made.append((high, rest, wide, product(wide if fine_cross else high, weights)))
            solved = []
            for i, (value, (high, rest, wide, turned)) in enumerate(zip(values, made)):
                right = product(wide, table[:, right_at + LANES * i : right_at + LANES * (i + 1)])
                stack = [high, rest.astype(jnp.bfloat16), high]
                for k in range(rank):
                    part = turned[:, LANES * k : LANES * (k + 1)]
                    part_high = part.astype(jnp.bfloat16)
                    stack.append(part_high)
                    if k < fine_cross:
                        stack += [(part - part_high.astype(jnp.float32)).astype(jnp.bfloat16), part_high]
                stack = jnp.concatenate(stack, 0)
                left = table[GRID * i : GRID * (i + 1), left_at : left_at + stack.shape[0]]
                solved.append((right, product(left, stack)))
            return solved

        def step(state, extra=None):
            sub, cat = state
            uptake = h * (sub * cat * cat)
            values = (sub + (supply - supply * sub - uptake), cat + (uptake - decay * cat))
            sums = [a + b for a, b in solve(values)]
            if extra is not None:
                sums = [a + b for a, b in zip(sums, extra)]
            return tuple(a + b for a, b in zip(values, sums))

        return step


FINE = Level(fine_step, 1, 0)
MIDDLE = Level(level_step, 1, 1)
COARSE = Level(coarse_step, 3, 1)
near_tables = np.concatenate([FINE.tables, MIDDLE.tables], 1)


def bound(fields, near_table, far_table=None):
    rates = loaded(fields.at[2:])
    fine, middle = FINE.bind(near_table, 0, *rates), MIDDLE.bind(near_table, FINE.width, *rates)
    return fine, middle, None if far_table is None else COARSE.bind(far_table, 0, *rates)


def fetch_kernel(source, target):
    target[...] = source[...]


def relax_kernel(far_ref, fields, near_table, share_ref, arrived_ref):
    fine, middle, _ = bound(fields, near_table)
    position = lax.axis_index("tm")
    first = loaded(fields)
    prior = choose(position == 1, first, loaded(far_ref))
    for _ in range(STEPS_DEV):
        prior = fine(prior)
    shifted = choose(position == 0, first, prior)
    leap = middle(shifted)
    arrived = shifted
    for _ in range(STEPS_DEV):
        arrived = fine(arrived)
    share_ref[...] = merge(choose(position % GROUP == 0, shifted, minus(arrived, leap)))
    arrived_ref[...] = merge(arrived)


def chain(step, load, state, start, stop, block, keep=None):
    def turn(t, state):
        for i in range(block):
            j = start + t * block + i
            state = step(state, spread(load(j)))
            if keep is not None:
                keep[j + 1] = merge(state)
        return state

    return lax.fori_loop(0, (stop - start) // block, turn, state)


def group_kernel(
    shares_ref, near_ref, arrived_ref, fields, near_table, far_table, first_ref, rhs_ref, half_ref, residual_ref
):
    fine, middle, coarse = bound(fields, near_table, far_table)
    position = lax.axis_index("tm")
    own = choose(position == 0, loaded(fields), loaded(near_ref))
    start = spread(shares_ref[0])
    state = start
    for _ in range(STEPS_DEV):
        state, own = fine(state), fine(own)
    unpack_to(residual_ref, minus(spread(arrived_ref[...]), own))
    leap, handed = middle(start), coarse(start)
    first_ref[...] = merge(minus(state, leap))
    state = chain(middle, lambda j: shares_ref[j], state, 1, GROUP, 5)
    rhs = merge(choose(position < GROUP, state, minus(state, handed)))
    rhs_ref[...] = rhs
    half_ref[...] = jnp.where(position % 2 == 0, rhs[: GRID // 2], rhs[GRID // 2 :])


def correct_kernel(
    sides_ref, rhs_ref, shares_ref, first_ref, fields, near_table, far_table,
    points_ref, value_ref, defect_ref, coarse_kept, middle_kept,
):
    fine, middle, coarse = bound(fields, near_table, far_table)
    position = lax.axis_index("tm")
    member, group_id = position % GROUP, position // GROUP

    def coarse_side(g):
        return jnp.concatenate([sides_ref[0, g], sides_ref[1, g]], 0)

    coarse_kept[0] = merge(loaded(fields))
    coarse_kept[1] = coarse_side(0)
    chain(coarse, coarse_side, spread(coarse_side(0)), 1, sides_ref.shape[1], 5, coarse_kept)
    earlier = spread(coarse_kept[group_id])
    own_side = spread(rhs_ref[...])
    value = choose(group_id == 0, own_side, coarse(earlier, own_side))
    unpack_to(value_ref.at[0], value)
    middle_kept[0] = merge(earlier)
    state = middle(earlier, spread(first_ref[...]))
    middle_kept[1] = merge(state)
    chain(middle, lambda j: shares_ref[j], state, 1, GROUP - 1, 7, middle_kept)
    prior = spread(middle_kept[member])
    side = spread(jnp.where(member == 0, first_ref[...], shares_ref[member]))
    updated = middle(prior, side)
    closing = member == GROUP - 1
    state = prior
    for i in range(STEPS_DEV - 1):
        state = fine(state)
        unpack_to(points_ref.at[i], state)
    unpack_to(points_ref.at[STEPS_DEV - 1], choose(closing, value, updated))
    unpack_to(defect_ref.at[0], choose(closing, minus(updated, value), minus(value, value)))


VMEM = pl.BlockSpec(memory_space=pltpu.VMEM)


def call(kernel, outs, in_specs, scratch, limit, *operands):
    return pl.pallas_call(
        kernel,
        out_shape=[jax.ShapeDtypeStruct(o, jnp.float32) for o in outs],
        in_specs=in_specs,
        out_specs=[VMEM] * len(outs),
        scratch_shapes=scratch,
        compiler_params=pltpu.CompilerParams(vmem_limit_bytes=limit * 2**20),
    )(*operands)


def shards(initial, coarse_guess, feed_rate, kill_rate):
    devices = lax.axis_size("tm")
    groups = devices // GROUP
    field, pair, half = (GRID, LANES), (2, GRID, GRID), (GRID // 2, LANES)
    own = coarse_guess[0]
    far = lax.ppermute(own, "tm", [(i, i + 2) for i in range(devices - 2)])
    far_table = jnp.asarray(COARSE.tables)
    fields = jnp.concatenate([initial, feed_rate[None], kill_rate[None]], 0)
    near_table = pl.pallas_call(
        fetch_kernel,
        out_shape=jax.ShapeDtypeStruct(near_tables.shape, jnp.bfloat16),
        in_specs=[VMEM],
        out_specs=VMEM,
        cost_estimate=pl.CostEstimate(flops=0, bytes_accessed=4 * near_tables.size, transcendentals=0),
        compiler_params=pltpu.CompilerParams(vmem_limit_bytes=16 * 2**20),
    )(jnp.asarray(near_tables))
    share, arrived = call(relax_kernel, [field, field], [VMEM] * 3, [], 16, far, fields, near_table)
    share, own = lax.optimization_barrier((share, own))
    near = lax.ppermute(own, "tm", [(i, i + 1) for i in range(devices - 1)])
    inside = [[g * GROUP + m for m in range(GROUP)] for g in range(groups)]
    shares = lax.all_gather(share, "tm", axis_index_groups=inside)
    first, rhs, part, residual = call(
        group_kernel,
        [field, field, half, pair],
        [VMEM] * 6,
        [],
        16,
        shares, near, arrived, fields, near_table, far_table,
    )
    across = [[g * GROUP + m for g in range(groups)] for m in range(GROUP)]
    parts = lax.all_to_all(jnp.broadcast_to(part[None], (groups,) + half), "tm", 0, 0, axis_index_groups=across)
    cores = [[2 * c, 2 * c + 1] for c in range(devices // 2)]
    sides = lax.all_gather(parts[: groups - 1], "tm", axis_index_groups=cores)
    points, value, defect = call(
        correct_kernel,
        [(STEPS_DEV,) + pair, (1,) + pair, (1,) + pair],
        [VMEM] * 7,
        [pltpu.VMEM((groups,) + field, jnp.float32), pltpu.VMEM((GROUP,) + field, jnp.float32)],
        16,
        sides, rhs, shares, first, fields, near_table, far_table,
    )
    return points, residual[None], value, defect


def solution(mesh):
    in_specs = (P(), P("tm", None, None, None), P(), P())
    out_specs = (P("tm", None, None, None),) * 4
    return jax.shard_map(shards, mesh=mesh, in_specs=in_specs, out_specs=out_specs, check_vma=False)
```

```python
import functools

import jax
import jax.numpy as jnp
import ml_dtypes
import numpy as np
from jax import lax
from jax.experimental import pallas as pl
from jax.experimental.pallas import tpu as pltpu
from jax.sharding import PartitionSpec as P

GRID = 64
GROUP = 16
STEPS_DEV = 4
LANES = 2 * GRID
diffusion = (0.2, 0.1)
interval_time = 0.03125
fine_step = interval_time / STEPS_DEV
level_step = interval_time
coarse_step = interval_time * GROUP


def basis_tables():
    positions = np.arange(GRID, dtype=np.float32)
    angles = np.float32(np.pi) * (positions[:, None] + np.float32(0.5)) * positions[None] / np.float32(GRID)
    weight = np.where(positions == 0, np.sqrt(np.float32(1 / GRID)), np.sqrt(np.float32(2 / GRID)))
    cosines = np.cos(angles.astype(np.float64)).astype(np.float32)
    basis = cosines * weight[None].astype(np.float32)
    sines = np.sin((np.float32(np.pi) * positions / np.float32(2 * GRID)).astype(np.float64)).astype(np.float32)
    return basis.astype(np.float64), (np.float32(-4) * sines * sines).astype(np.float64)


def solve_terms(time_step, rate, rank):
    basis, values = basis_tables()
    inverse = 1 / (1 - time_step * rate * (values[:, None] + values[None]))
    side = inverse[:, 0] - 1
    rest = inverse - 1 - side[:, None] - side[None]
    weights, vectors = np.linalg.eigh(rest)
    order = np.argsort(-np.abs(weights))[:rank]
    first = (basis * side) @ basis.T + basis @ basis.T - np.eye(GRID)
    cross = [(basis * (vectors[:, k] * np.sqrt(np.abs(weights[k])))) @ basis.T for k in order]
    return first, cross, [np.sign(weights[k]) for k in order]


def halves(matrix):
    high = matrix.astype(np.float32).astype(ml_dtypes.bfloat16)
    low = (matrix - high.astype(np.float64)).astype(np.float32).astype(ml_dtypes.bfloat16)
    return high, low


def twice(matrix):
    return np.concatenate([matrix, matrix], 1)


def species_tables(time_step, rate, rank, fine_cross):
    first, cross, signs = solve_terms(time_step, rate, rank)
    high, low = halves(first)
    right = np.concatenate([twice(high), twice(high), twice(low), np.zeros_like(twice(low))], 0)
    left = [high, high, low]
    cross_high, cross_low = zip(*[halves(m) for m in cross])
    cross_high = np.concatenate([twice(m) for m in cross_high], 1)
    cross_low = np.concatenate([twice(m) for m in cross_low], 1)
    parts = [cross_high, cross_high, cross_low] if fine_cross else [cross_high, cross_low]
    blank = np.zeros((4 * GRID - GRID * len(parts), cross_high.shape[1]), ml_dtypes.bfloat16)
    mixing = np.concatenate(parts + [blank], 0)
    for k, (matrix, sign) in enumerate(zip(cross, signs)):
        high, low = halves(matrix * sign)
        left += [high, high, low] if k < fine_cross else [high]
    return right, mixing, np.concatenate(left, 1)


@functools.lru_cache(None)
def level_tables(time_step, rank, fine_cross):
    sub = species_tables(time_step, diffusion[0], rank, fine_cross)
    cat = species_tables(time_step, diffusion[1], rank, fine_cross)
    left = np.concatenate([sub[2], cat[2]], 0)
    left = np.concatenate([left, np.zeros_like(left)], 0)
    return np.concatenate([sub[0], sub[1], cat[0], cat[1], left], 1)


def product(left, right):
    return jnp.dot(left, right, preferred_element_type=jnp.float32)


def second_half():
    return lax.broadcasted_iota(jnp.int32, (GRID, LANES), 1) >= GRID


def spread(fields):
    turned = pltpu.roll(fields, GRID, 1)
    second = second_half()
    return jnp.where(second, turned, fields), jnp.where(second, fields, turned)


def merge(state):
    return jnp.where(second_half(), state[1], state[0])


def loaded(pair):
    return tuple(jnp.concatenate([pair[i], pair[i]], 1) for i in range(2))


def unpack_to(ref, state):
    ref[0] = state[0][:, :GRID]
    ref[1] = state[1][:, :GRID]


def choose(condition, one, other):
    return tuple(jnp.where(condition, a, b) for a, b in zip(one, other))


def plus(one, other):
    return tuple(a + b for a, b in zip(one, other))


def minus(one, other):
    return tuple(a - b for a, b in zip(one, other))


class Level:
    def __init__(self, time_step, rank, fine_cross):
        self.time_step, self.rank, self.fine_cross = time_step, rank, fine_cross
        self.tables = level_tables(time_step, rank, fine_cross)
        self.width = self.tables.shape[1]

    def bind(self, table, start, feed, kill):
        h = jnp.float32(self.time_step)
        rank, fine_cross = self.rank, self.fine_cross
        cross = LANES * rank
        second = second_half()
        supply, decay = h * feed, h * (feed + kill)
        wide_at = [start, start + LANES + cross]
        left_at = start + 2 * (LANES + cross)

        def solve(values):
            count = values[0].shape[0] // GRID
            halves_of = second if count == 1 else jnp.concatenate([second] * count, 0)
            rows = [slice(GRID * n, GRID * (n + 1)) for n in range(count)]
            made = []
            for i, value in enumerate(values):
                high = value.astype(jnp.bfloat16)
                rest = value - high.astype(jnp.float32)
                mixed = jnp.where(halves_of, rest, value).astype(jnp.bfloat16)
                wide = jnp.concatenate([mixed, high], 1)
                at, stop = wide_at[i], wide_at[i] + LANES + cross
                if fine_cross:
                    right = product(wide, table[:, at:stop])
                    right, turned = right[:, :LANES], right[:, LANES:]
                else:
                    turned = product(high, table[: 2 * GRID, at + LANES : stop])
                    right = None
                made.append((high, rest, wide, turned, right))
            solved = []
            for i, (high, rest, wide, turned, right) in enumerate(made):
                if not fine_cross:
                    right = product(wide, table[:, wide_at[i] : wide_at[i] + LANES])
                stack = [high, rest.astype(jnp.bfloat16), high]
                for k in range(rank):
                    part = turned[:, LANES * k : LANES * (k + 1)]
                    part_high = part.astype(jnp.bfloat16)
                    stack.append(part_high)
                    if k < fine_cross:
                        stack += [(part - part_high.astype(jnp.float32)).astype(jnp.bfloat16), part_high]
                stack = jnp.concatenate([jnp.concatenate([p[r] for p in stack], 0) for r in rows], 1)
                left = product(table[GRID * i : GRID * (i + 1), left_at : left_at + stack.shape[0]], stack)
                left = jnp.concatenate([left[:, LANES * n : LANES * (n + 1)] for n in range(count)], 0)
                solved.append((right, left))
            return solved

        def react(state):
            sub, cat = state
            uptake = h * (sub * cat * cat)
            return sub + (supply - supply * sub - uptake), cat + (uptake - decay * cat)

        def step(state, extra=None):
            values = react(state)
            sums = [a + b for a, b in solve(values)]
            if extra is not None:
                sums = [a + b for a, b in zip(sums, extra)]
            return tuple(a + b for a, b in zip(values, sums))

        def step_two(one, other):
            values = [jnp.concatenate(pair, 0) for pair in zip(react(one), react(other))]
            values = [a + (b + c) for a, (b, c) in zip(values, solve(values))]
            return tuple(v[:GRID] for v in values), tuple(v[GRID:] for v in values)

        step.two = step_two
        return step


FINE = Level(fine_step, 1, 0)
MIDDLE = Level(level_step, 1, 1)
COARSE = Level(coarse_step, 3, 1)
near_tables = np.concatenate([FINE.tables, MIDDLE.tables], 1)


def bound(fields, near_table, far_table=None):
    rates = loaded(fields.at[2:4])
    fine, middle = FINE.bind(near_table, 0, *rates), MIDDLE.bind(near_table, FINE.width, *rates)
    return fine, middle, None if far_table is None else COARSE.bind(far_table, 0, *rates)


def fetch_kernel(source, target):
    target[...] = source[...]


def relax_kernel(far_ref, fields, near_table, share_ref, arrived_ref, swap_ref):
    fine, middle, _ = bound(fields, near_table)
    position = lax.axis_index("tm")
    first = loaded(fields)
    sent = choose(position % 2 == 0, loaded(fields.at[4:]), loaded(far_ref))
    swap_ref[...] = merge(sent)
    prior = choose(position == 1, first, loaded(far_ref))
    for _ in range(STEPS_DEV):
        prior = fine(prior)
    shifted = choose(position == 0, first, prior)
    leap = middle(shifted)
    arrived = shifted
    for _ in range(STEPS_DEV):
        arrived = fine(arrived)
    share_ref[...] = merge(choose(position % GROUP == 0, shifted, minus(arrived, leap)))
    arrived_ref[...] = merge(arrived)


def chain(step, load, state, start, stop, block, keep=None):
    def turn(t, state):
        for i in range(block):
            j = start + t * block + i
            state = step(state, spread(load(j)))
            if keep is not None:
                keep[j + 1] = merge(state)
        return state

    return lax.fori_loop(0, (stop - start) // block, turn, state)


def group_kernel(
    shares_ref, near_ref, arrived_ref, fields, near_table, far_table, first_ref, rhs_ref, half_ref, residual_ref
):
    fine, middle, coarse = bound(fields, near_table, far_table)
    position = lax.axis_index("tm")
    own = choose(position == 0, loaded(fields), spread(near_ref[...]))
    start = spread(shares_ref[0])
    state = start
    for _ in range(STEPS_DEV):
        state, own = fine.two(state, own)
    unpack_to(residual_ref, minus(spread(arrived_ref[...]), own))
    leap, handed = middle(start), coarse(start)
    first_ref[...] = merge(minus(state, leap))
    state = chain(middle, lambda j: shares_ref[j], state, 1, GROUP, 5)
    rhs = merge(choose(position < GROUP, state, minus(state, handed)))
    rhs_ref[...] = rhs
    half_ref[...] = jnp.where(position % 2 == 0, rhs[: GRID // 2], rhs[GRID // 2 :])


def correct_kernel(
    sides_ref, rhs_ref, shares_ref, first_ref, fields, near_table, far_table,
    points_ref, value_ref, defect_ref, coarse_kept, middle_kept,
):
    fine, middle, coarse = bound(fields, near_table, far_table)
    position = lax.axis_index("tm")
    member, group_id = position % GROUP, position // GROUP

    def coarse_side(g):
        return jnp.concatenate([sides_ref[0, g], sides_ref[1, g]], 0)

    coarse_kept[0] = merge(loaded(fields))
    coarse_kept[1] = coarse_side(0)
    chain(coarse, coarse_side, spread(coarse_side(0)), 1, sides_ref.shape[1], 5, coarse_kept)
    earlier = spread(coarse_kept[group_id])
    own_side = spread(rhs_ref[...])
    value = choose(group_id == 0, own_side, coarse(earlier, own_side))
    unpack_to(value_ref.at[0], value)
    middle_kept[0] = merge(earlier)
    state = middle(earlier, spread(first_ref[...]))
    middle_kept[1] = merge(state)
    chain(middle, lambda j: shares_ref[j], state, 1, GROUP - 1, 7, middle_kept)
    prior = spread(middle_kept[member])
    side = spread(jnp.where(member == 0, first_ref[...], shares_ref[member]))
    updated = middle(prior, side)
    closing = member == GROUP - 1
    state = prior
    for i in range(STEPS_DEV - 1):
        state = fine(state)
        unpack_to(points_ref.at[i], state)
    unpack_to(points_ref.at[STEPS_DEV - 1], choose(closing, value, updated))
    unpack_to(defect_ref.at[0], choose(closing, minus(updated, value), minus(value, value)))


VMEM = pl.BlockSpec(memory_space=pltpu.VMEM)


def call(kernel, outs, in_specs, scratch, limit, *operands):
    return pl.pallas_call(
        kernel,
        out_shape=[jax.ShapeDtypeStruct(o, jnp.float32) for o in outs],
        in_specs=in_specs,
        out_specs=[VMEM] * len(outs),
        scratch_shapes=scratch,
        compiler_params=pltpu.CompilerParams(vmem_limit_bytes=limit * 2**20),
    )(*operands)


def shards(initial, coarse_guess, feed_rate, kill_rate):
    devices = lax.axis_size("tm")
    groups = devices // GROUP
    field, pair, half = (GRID, LANES), (2, GRID, GRID), (GRID // 2, LANES)
    own = coarse_guess[0]
    far = lax.ppermute(own, "tm", [(i, i + 2) for i in range(devices - 2)])
    far_table = jnp.asarray(COARSE.tables)
    fields = jnp.concatenate([initial, feed_rate[None], kill_rate[None], own], 0)
    near_table = pl.pallas_call(
        fetch_kernel,
        out_shape=jax.ShapeDtypeStruct(near_tables.shape, jnp.bfloat16),
        in_specs=[VMEM],
        out_specs=VMEM,
        cost_estimate=pl.CostEstimate(flops=0, bytes_accessed=4 * near_tables.size, transcendentals=0),
        compiler_params=pltpu.CompilerParams(vmem_limit_bytes=16 * 2**20),
    )(jnp.asarray(near_tables))
    share, arrived, swap = call(relax_kernel, [field] * 3, [VMEM] * 3, [], 16, far, fields, near_table)
    near = lax.ppermute(swap, "tm", [(i, i ^ 1) for i in range(devices)])
    inside = [[g * GROUP + m for m in range(GROUP)] for g in range(groups)]
    shares = lax.all_gather(share, "tm", axis_index_groups=inside)
    first, rhs, part, residual = call(
        group_kernel,
        [field, field, half, pair],
        [VMEM] * 6,
        [],
        16,
        shares, near, arrived, fields, near_table, far_table,
    )
    across = [[g * GROUP + m for g in range(groups)] for m in range(GROUP)]
    parts = lax.all_to_all(jnp.broadcast_to(part[None], (groups,) + half), "tm", 0, 0, axis_index_groups=across)
    cores = [[2 * c, 2 * c + 1] for c in range(devices // 2)]
    sides = lax.all_gather(parts[: groups - 1], "tm", axis_index_groups=cores)
    points, value, defect = call(
        correct_kernel,
        [(STEPS_DEV,) + pair, (1,) + pair, (1,) + pair],
        [VMEM] * 7,
        [pltpu.VMEM((groups,) + field, jnp.float32), pltpu.VMEM((GROUP,) + field, jnp.float32)],
        16,
        sides, rhs, shares, first, fields, near_table, far_table,
    )
    return points, residual[None], value, defect


def solution(mesh):
    in_specs = (P(), P("tm", None, None, None), P(), P())
    out_specs = (P("tm", None, None, None),) * 4
    return jax.shard_map(shards, mesh=mesh, in_specs=in_specs, out_specs=out_specs, check_vma=False)
```

```python
import functools

import jax
import jax.numpy as jnp
import ml_dtypes
import numpy as np
from jax import lax
from jax.experimental import pallas as pl
from jax.experimental.pallas import tpu as pltpu
from jax.sharding import PartitionSpec as P

GRID = 64
GROUP = 16
STEPS_DEV = 4
LANES = 2 * GRID
diffusion = (0.2, 0.1)
interval_time = 0.03125
fine_step = interval_time / STEPS_DEV
level_step = interval_time
coarse_step = interval_time * GROUP


def basis_tables():
    positions = np.arange(GRID, dtype=np.float32)
    angles = np.float32(np.pi) * (positions[:, None] + np.float32(0.5)) * positions[None] / np.float32(GRID)
    weight = np.where(positions == 0, np.sqrt(np.float32(1 / GRID)), np.sqrt(np.float32(2 / GRID)))
    cosines = np.cos(angles.astype(np.float64)).astype(np.float32)
    basis = cosines * weight[None].astype(np.float32)
    sines = np.sin((np.float32(np.pi) * positions / np.float32(2 * GRID)).astype(np.float64)).astype(np.float32)
    return basis.astype(np.float64), (np.float32(-4) * sines * sines).astype(np.float64)


def solve_terms(time_step, rate, rank):
    basis, values = basis_tables()
    inverse = 1 / (1 - time_step * rate * (values[:, None] + values[None]))
    side = inverse[:, 0] - 1
    rest = inverse - 1 - side[:, None] - side[None]
    weights, vectors = np.linalg.eigh(rest)
    order = np.argsort(-np.abs(weights))[:rank]
    first = (basis * side) @ basis.T + basis @ basis.T - np.eye(GRID)
    cross = [(basis * (vectors[:, k] * np.sqrt(np.abs(weights[k])))) @ basis.T for k in order]
    return first, cross, [np.sign(weights[k]) for k in order]


def halves(matrix):
    high = matrix.astype(np.float32).astype(ml_dtypes.bfloat16)
    low = (matrix - high.astype(np.float64)).astype(np.float32).astype(ml_dtypes.bfloat16)
    return high, low


def twice(matrix):
    return np.concatenate([matrix, matrix], 1)


def species_tables(time_step, rate, rank, fine_cross):
    first, cross, signs = solve_terms(time_step, rate, rank)
    high, low = halves(first)
    right = np.concatenate([twice(high), twice(high), twice(low), np.zeros_like(twice(low))], 0)
    left = [high, high, low]
    cross_high, cross_low = zip(*[halves(m) for m in cross])
    cross_high = np.concatenate([twice(m) for m in cross_high], 1)
    cross_low = np.concatenate([twice(m) for m in cross_low], 1)
    parts = [cross_high, cross_high, cross_low] if fine_cross else [cross_high, cross_low]
    blank = np.zeros((4 * GRID - GRID * len(parts), cross_high.shape[1]), ml_dtypes.bfloat16)
    mixing = np.concatenate(parts + [blank], 0)
    for k, (matrix, sign) in enumerate(zip(cross, signs)):
        high, low = halves(matrix * sign)
        left += [high, high, low] if k < fine_cross else [high]
    return right, mixing, np.concatenate(left, 1)


@functools.lru_cache(None)
def level_tables(time_step, rank, fine_cross):
    sub = species_tables(time_step, diffusion[0], rank, fine_cross)
    cat = species_tables(time_step, diffusion[1], rank, fine_cross)
    left = np.concatenate([sub[2], cat[2]], 0)
    left = np.concatenate([left, np.zeros_like(left)], 0)
    return np.concatenate([sub[0], sub[1], cat[0], cat[1], left], 1)


def product(left, right):
    return jnp.dot(left, right, preferred_element_type=jnp.float32)


def second_half():
    return lax.broadcasted_iota(jnp.int32, (GRID, LANES), 1) >= GRID


def spread(fields):
    turned = pltpu.roll(fields, GRID, 1)
    second = second_half()
    return jnp.where(second, turned, fields), jnp.where(second, fields, turned)


def merge(state):
    return jnp.where(second_half(), state[1], state[0])


def loaded(pair):
    return tuple(jnp.concatenate([pair[i], pair[i]], 1) for i in range(2))


def unpack_to(ref, state):
    ref[0] = state[0][:, :GRID]
    ref[1] = state[1][:, :GRID]


def choose(condition, one, other):
    return tuple(jnp.where(condition, a, b) for a, b in zip(one, other))


def plus(one, other):
    return tuple(a + b for a, b in zip(one, other))


def minus(one, other):
    return tuple(a - b for a, b in zip(one, other))


class Level:
    def __init__(self, time_step, rank, fine_cross):
        self.time_step, self.rank, self.fine_cross = time_step, rank, fine_cross
        self.tables = level_tables(time_step, rank, fine_cross)
        self.width = self.tables.shape[1]

    def bind(self, table, start, feed, kill):
        h = jnp.float32(self.time_step)
        rank, fine_cross = self.rank, self.fine_cross
        cross = LANES * rank
        second = second_half()
        supply, decay = h * feed, h * (feed + kill)
        wide_at = [start, start + LANES + cross]
        left_at = start + 2 * (LANES + cross)

        def solve(values):
            count = values[0].shape[0] // GRID
            halves_of = second if count == 1 else jnp.concatenate([second] * count, 0)
            rows = [slice(GRID * n, GRID * (n + 1)) for n in range(count)]
            made = []
            for i, value in enumerate(values):
                high = value.astype(jnp.bfloat16)
                rest = value - high.astype(jnp.float32)
                mixed = jnp.where(halves_of, rest, value).astype(jnp.bfloat16)
                wide = jnp.concatenate([mixed, high], 1)
                at, stop = wide_at[i], wide_at[i] + LANES + cross
                if fine_cross:
                    right = product(wide, table[:, at:stop])
                    right, turned = right[:, :LANES], right[:, LANES:]
                else:
                    turned = product(high, table[: 2 * GRID, at + LANES : stop])
                    right = None
                made.append((high, rest, wide, turned, right))
            solved = []
            for i, (high, rest, wide, turned, right) in enumerate(made):
                if not fine_cross:
                    right = product(wide, table[:, wide_at[i] : wide_at[i] + LANES])
                stack = [high, rest.astype(jnp.bfloat16), high]
                for k in range(rank):
                    part = turned[:, LANES * k : LANES * (k + 1)]
                    part_high = part.astype(jnp.bfloat16)
                    stack.append(part_high)
                    if k < fine_cross:
                        stack += [(part - part_high.astype(jnp.float32)).astype(jnp.bfloat16), part_high]
                stack = jnp.concatenate([jnp.concatenate([p[r] for p in stack], 0) for r in rows], 1)
                left = product(table[GRID * i : GRID * (i + 1), left_at : left_at + stack.shape[0]], stack)
                left = jnp.concatenate([left[:, LANES * n : LANES * (n + 1)] for n in range(count)], 0)
                solved.append((right, left))
            return solved

        def react(state):
            sub, cat = state
            uptake = h * (sub * cat * cat)
            return sub + (supply - supply * sub - uptake), cat + (uptake - decay * cat)

        def step(state, extra=None):
            values = react(state)
            sums = [a + b for a, b in solve(values)]
            if extra is not None:
                sums = [a + b for a, b in zip(sums, extra)]
            return tuple(a + b for a, b in zip(values, sums))

        def step_two(one, other):
            values = [jnp.concatenate(pair, 0) for pair in zip(react(one), react(other))]
            values = [a + (b + c) for a, (b, c) in zip(values, solve(values))]
            return tuple(v[:GRID] for v in values), tuple(v[GRID:] for v in values)

        step.two = step_two
        return step


FINE = Level(fine_step, 1, 0)
MIDDLE = Level(level_step, 1, 1)
COARSE = Level(coarse_step, 3, 1)
near_tables = np.concatenate([FINE.tables, MIDDLE.tables], 1)


def bound(fields, near_table, far_table=None):
    rates = loaded(fields.at[2:4])
    fine, middle = FINE.bind(near_table, 0, *rates), MIDDLE.bind(near_table, FINE.width, *rates)
    return fine, middle, None if far_table is None else COARSE.bind(far_table, 0, *rates)


def fetch_kernel(source, target):
    target[...] = source[...]


def relax_kernel(far_ref, fields, near_table, share_ref, arrived_ref):
    fine, middle, _ = bound(fields, near_table)
    position = lax.axis_index("tm")
    first = loaded(fields)
    prior = choose(position == 1, first, loaded(far_ref))
    for _ in range(STEPS_DEV):
        prior = fine(prior)
    shifted = choose(position == 0, first, prior)
    leap = middle(shifted)
    arrived = shifted
    for _ in range(STEPS_DEV):
        arrived = fine(arrived)
    share_ref[...] = merge(choose(position % GROUP == 0, shifted, minus(arrived, leap)))
    arrived_ref[...] = merge(arrived)


def chain(step, load, state, start, stop, block, keep=None):
    def turn(t, state):
        for i in range(block):
            j = start + t * block + i
            state = step(state, spread(load(j)))
            if keep is not None:
                keep[j + 1] = merge(state)
        return state

    return lax.fori_loop(0, (stop - start) // block, turn, state)


def group_kernel(
    shares_ref, near_ref, arrived_ref, fields, near_table, far_table,
    first_ref, rhs_ref, parts_ref, residual_out, residual_ref, sems,
):
    fine, middle, coarse = bound(fields, near_table, far_table)
    position = lax.axis_index("tm")
    own = choose(position == 0, loaded(fields), loaded(near_ref))
    start = spread(shares_ref[0])
    state = start
    for _ in range(STEPS_DEV):
        state, own = fine.two(state, own)
    unpack_to(residual_ref, minus(spread(arrived_ref[...]), own))
    residual_copy = pltpu.make_async_copy(residual_ref, residual_out, sems.at[0])
    residual_copy.start()
    leap, handed = middle(start), coarse(start)
    first_ref[...] = merge(minus(state, leap))
    state = chain(middle, lambda j: shares_ref[j], state, 1, GROUP, 5)
    rhs = merge(choose(position < GROUP, state, minus(state, handed)))
    rhs_ref[...] = rhs
    part = jnp.where(position % 2 == 0, rhs[: GRID // 2], rhs[GRID // 2 :])
    for g in range(parts_ref.shape[0]):
        parts_ref[g] = part
    residual_copy.wait()


def correct_kernel(
    sides_ref, rhs_ref, shares_ref, first_ref, fields, near_table, far_table,
    points_out, value_out, defect_out, points_ref, value_ref, defect_ref, coarse_kept, middle_kept, sems,
):
    fine, middle, coarse = bound(fields, near_table, far_table)
    position = lax.axis_index("tm")
    member, group_id = position % GROUP, position // GROUP

    def coarse_side(g):
        return jnp.concatenate([sides_ref[0, g], sides_ref[1, g]], 0)

    coarse_kept[0] = merge(loaded(fields))
    coarse_kept[1] = coarse_side(0)
    chain(coarse, coarse_side, spread(coarse_side(0)), 1, sides_ref.shape[1], 5, coarse_kept)
    earlier = spread(coarse_kept[group_id])
    own_side = spread(rhs_ref[...])
    value = choose(group_id == 0, own_side, coarse(earlier, own_side))
    copies = []

    def emit(source, target):
        copies.append(pltpu.make_async_copy(source, target, sems.at[len(copies)]))
        copies[-1].start()

    unpack_to(value_ref, value)
    emit(value_ref, value_out.at[0])
    middle_kept[0] = merge(earlier)
    state = middle(earlier, spread(first_ref[...]))
    middle_kept[1] = merge(state)
    chain(middle, lambda j: shares_ref[j], state, 1, GROUP - 1, 7, middle_kept)
    prior = spread(middle_kept[member])
    side = spread(jnp.where(member == 0, first_ref[...], shares_ref[member]))
    updated = middle(prior, side)
    closing = member == GROUP - 1
    unpack_to(points_ref.at[STEPS_DEV - 1], choose(closing, value, updated))
    emit(points_ref.at[STEPS_DEV - 1], points_out.at[STEPS_DEV - 1])
    unpack_to(defect_ref, choose(closing, minus(updated, value), minus(value, value)))
    emit(defect_ref, defect_out.at[0])
    state = prior
    for i in range(STEPS_DEV - 1):
        state = fine(state)
        unpack_to(points_ref.at[i], state)
        emit(points_ref.at[i], points_out.at[i])
    for copy in copies:
        copy.wait()


VMEM = pl.BlockSpec(memory_space=pltpu.VMEM)
HBM = pl.BlockSpec(memory_space=pltpu.HBM)


def call(kernel, shapes, in_specs, out_specs, scratch, *operands):
    return pl.pallas_call(
        kernel,
        out_shape=[jax.ShapeDtypeStruct(s, jnp.float32) for s in shapes],
        in_specs=in_specs,
        out_specs=out_specs,
        scratch_shapes=scratch,
        compiler_params=pltpu.CompilerParams(vmem_limit_bytes=16 * 2**20),
    )(*operands)


def shards(initial, coarse_guess, feed_rate, kill_rate):
    devices = lax.axis_size("tm")
    groups = devices // GROUP
    field, pair, half = (GRID, LANES), (2, GRID, GRID), (GRID // 2, LANES)
    own = coarse_guess[0]
    far = lax.ppermute(own, "tm", [(i, i + 2) for i in range(devices - 2)])
    far_table = jnp.asarray(COARSE.tables)
    fields = jnp.concatenate([initial, feed_rate[None], kill_rate[None]], 0)
    near_table = pl.pallas_call(
        fetch_kernel,
        out_shape=jax.ShapeDtypeStruct(near_tables.shape, jnp.bfloat16),
        in_specs=[VMEM],
        out_specs=VMEM,
        cost_estimate=pl.CostEstimate(flops=0, bytes_accessed=4 * near_tables.size, transcendentals=0),
        compiler_params=pltpu.CompilerParams(vmem_limit_bytes=16 * 2**20),
    )(jnp.asarray(near_tables))
    near_table, own = lax.optimization_barrier((near_table, own))
    near = lax.ppermute(own, "tm", [(i, i + 1) for i in range(devices - 1)])
    share, arrived = call(relax_kernel, [field] * 2, [VMEM] * 3, [VMEM] * 2, [], far, fields, near_table)
    inside = [[g * GROUP + m for m in range(GROUP)] for g in range(groups)]
    shares = lax.all_gather(share, "tm", axis_index_groups=inside)
    parts_shape = (groups,) + half
    first, rhs, parts, residual = call(
        group_kernel,
        [field, field, parts_shape, pair],
        [VMEM] * 6,
        [VMEM] * 3 + [HBM],
        [pltpu.VMEM(pair, jnp.float32), pltpu.SemaphoreType.DMA((1,))],
        shares, near, arrived, fields, near_table, far_table,
    )
    across = [[g * GROUP + m for g in range(groups)] for m in range(GROUP)]
    parts = lax.all_to_all(parts, "tm", 0, 0, axis_index_groups=across)
    cores = [[2 * c, 2 * c + 1] for c in range(devices // 2)]
    sides = lax.all_gather(parts[: groups - 1], "tm", axis_index_groups=cores)
    shapes = [(STEPS_DEV,) + pair, pair, pair, (groups,) + field, (GROUP,) + field]
    points, value, defect = call(
        correct_kernel,
        [(STEPS_DEV,) + pair, (1,) + pair, (1,) + pair],
        [VMEM] * 7,
        [HBM] * 3,
        [pltpu.VMEM(s, jnp.float32) for s in shapes] + [pltpu.SemaphoreType.DMA((STEPS_DEV + 2,))],
        sides, rhs, shares, first, fields, near_table, far_table,
    )
    return points, residual[None], value, defect


def solution(mesh):
    in_specs = (P(), P("tm", None, None, None), P(), P())
    out_specs = (P("tm", None, None, None),) * 4
    return jax.shard_map(shards, mesh=mesh, in_specs=in_specs, out_specs=out_specs, check_vma=False)
```

```python
import functools

import jax
import jax.numpy as jnp
import ml_dtypes
import numpy as np
from jax import lax
from jax.experimental import pallas as pl
from jax.experimental.pallas import tpu as pltpu
from jax.sharding import PartitionSpec as P

GRID = 64
GROUP = 16
STEPS_DEV = 4
LANES = 2 * GRID
diffusion = (0.2, 0.1)
interval_time = 0.03125
fine_step = interval_time / STEPS_DEV
level_step = interval_time
coarse_step = interval_time * GROUP


def basis_tables():
    positions = np.arange(GRID, dtype=np.float32)
    angles = np.float32(np.pi) * (positions[:, None] + np.float32(0.5)) * positions[None] / np.float32(GRID)
    weight = np.where(positions == 0, np.sqrt(np.float32(1 / GRID)), np.sqrt(np.float32(2 / GRID)))
    cosines = np.cos(angles.astype(np.float64)).astype(np.float32)
    basis = cosines * weight[None].astype(np.float32)
    sines = np.sin((np.float32(np.pi) * positions / np.float32(2 * GRID)).astype(np.float64)).astype(np.float32)
    return basis.astype(np.float64), (np.float32(-4) * sines * sines).astype(np.float64)


def solve_terms(time_step, rate, rank):
    basis, values = basis_tables()
    inverse = 1 / (1 - time_step * rate * (values[:, None] + values[None]))
    side = inverse[:, 0] - 1
    rest = inverse - 1 - side[:, None] - side[None]
    weights, vectors = np.linalg.eigh(rest)
    order = np.argsort(-np.abs(weights))[:rank]
    first = (basis * side) @ basis.T + basis @ basis.T - np.eye(GRID)
    cross = [(basis * (vectors[:, k] * np.sqrt(np.abs(weights[k])))) @ basis.T for k in order]
    return first, cross, [np.sign(weights[k]) for k in order]


def halves(matrix):
    high = matrix.astype(np.float32).astype(ml_dtypes.bfloat16)
    low = (matrix - high.astype(np.float64)).astype(np.float32).astype(ml_dtypes.bfloat16)
    return high, low


def twice(matrix):
    return np.concatenate([matrix, matrix], 1)


def species_tables(time_step, rate, rank, fine_cross):
    first, cross, signs = solve_terms(time_step, rate, rank)
    high, low = halves(first)
    right = np.concatenate([twice(high), twice(low), twice(high), np.zeros_like(twice(low))], 0)
    left = [high, high, low]
    cross_high, cross_low = zip(*[halves(m) for m in cross])
    cross_high = np.concatenate([twice(m) for m in cross_high], 1)
    cross_low = np.concatenate([twice(m) for m in cross_low], 1)
    parts = [cross_high, cross_low, cross_high] if fine_cross else [cross_high, cross_low]
    blank = np.zeros((4 * GRID - GRID * len(parts), cross_high.shape[1]), ml_dtypes.bfloat16)
    mixing = np.concatenate(parts + [blank], 0)
    for k, (matrix, sign) in enumerate(zip(cross, signs)):
        high, low = halves(matrix * sign)
        left += [high, high, low] if k < fine_cross else [high]
    return right, mixing, np.concatenate(left, 1)


@functools.lru_cache(None)
def level_tables(time_step, rank, fine_cross):
    sub = species_tables(time_step, diffusion[0], rank, fine_cross)
    cat = species_tables(time_step, diffusion[1], rank, fine_cross)
    left = np.concatenate([sub[2], cat[2]], 0)
    left = np.concatenate([left, np.zeros_like(left)], 0)
    return np.concatenate([sub[0], sub[1], cat[0], cat[1], left], 1)


def product(left, right):
    return jnp.dot(left, right, preferred_element_type=jnp.float32)


def second_half():
    return lax.broadcasted_iota(jnp.int32, (GRID, LANES), 1) >= GRID


def spread(fields):
    turned = pltpu.roll(fields, GRID, 1)
    second = second_half()
    return jnp.where(second, turned, fields), jnp.where(second, fields, turned)


def merge(state):
    return jnp.where(second_half(), state[1], state[0])


def loaded(pair):
    return tuple(jnp.concatenate([pair[i], pair[i]], 1) for i in range(2))


def unpack_to(ref, state):
    ref[0] = state[0][:, :GRID]
    ref[1] = state[1][:, :GRID]


def choose(condition, one, other):
    return tuple(jnp.where(condition, a, b) for a, b in zip(one, other))


def plus(one, other):
    return tuple(a + b for a, b in zip(one, other))


def minus(one, other):
    return tuple(a - b for a, b in zip(one, other))


class Level:
    def __init__(self, time_step, rank, fine_cross):
        self.time_step, self.rank, self.fine_cross = time_step, rank, fine_cross
        self.tables = level_tables(time_step, rank, fine_cross)
        self.width = self.tables.shape[1]

    def bind(self, table, start, feed, kill):
        h = jnp.float32(self.time_step)
        rank, fine_cross = self.rank, self.fine_cross
        cross = LANES * rank
        supply, decay = h * feed, h * (feed + kill)
        wide_at = [start, start + LANES + cross]
        left_at = start + 2 * (LANES + cross)

        def solve(values):
            count = values[0].shape[0] // GRID
            rows = [slice(GRID * n, GRID * (n + 1)) for n in range(count)]
            made = []
            for i, value in enumerate(values):
                high = value.astype(jnp.bfloat16)
                rest = (value - high.astype(jnp.float32)).astype(jnp.bfloat16)
                wide = jnp.concatenate([high, rest], 1)
                at, stop = wide_at[i], wide_at[i] + LANES + cross
                if fine_cross:
                    right = product(wide, table[:, at:stop])
                    right, turned = right[:, :LANES], right[:, LANES:]
                else:
                    turned = product(high, table[: 2 * GRID, at + LANES : stop])
                    right = None
                made.append((high, rest, wide, turned, right))
            solved = []
            for i, (high, rest, wide, turned, right) in enumerate(made):
                if not fine_cross:
                    right = product(wide, table[:, wide_at[i] : wide_at[i] + LANES])
                stack = [high, rest, high]
                for k in range(rank):
                    part = turned[:, LANES * k : LANES * (k + 1)]
                    part_high = part.astype(jnp.bfloat16)
                    stack.append(part_high)
                    if k < fine_cross:
                        stack += [(part - part_high.astype(jnp.float32)).astype(jnp.bfloat16), part_high]
                stack = jnp.concatenate([jnp.concatenate([p[r] for p in stack], 0) for r in rows], 1)
                left = product(table[GRID * i : GRID * (i + 1), left_at : left_at + stack.shape[0]], stack)
                left = jnp.concatenate([left[:, LANES * n : LANES * (n + 1)] for n in range(count)], 0)
                solved.append((right, left))
            return solved

        def react(state):
            sub, cat = state
            uptake = (h * sub) * (cat * cat)
            return sub + (supply - supply * sub - uptake), cat + (uptake - decay * cat)

        def step(state, extra=None):
            values = react(state)
            sums = [a + b for a, b in solve(values)]
            if extra is not None:
                sums = [a + b for a, b in zip(sums, extra)]
            return tuple(a + b for a, b in zip(values, sums))

        def step_two(one, other):
            values = [jnp.concatenate(pair, 0) for pair in zip(react(one), react(other))]
            values = [a + (b + c) for a, (b, c) in zip(values, solve(values))]
            return tuple(v[:GRID] for v in values), tuple(v[GRID:] for v in values)

        step.two = step_two
        return step


FINE = Level(fine_step, 1, 0)
MIDDLE = Level(level_step, 1, 1)
COARSE = Level(coarse_step, 3, 1)
near_tables = np.concatenate([FINE.tables, MIDDLE.tables], 1)


def bound(fields, near_table, far_table=None):
    rates = loaded(fields.at[2:4])
    fine, middle = FINE.bind(near_table, 0, *rates), MIDDLE.bind(near_table, FINE.width, *rates)
    return fine, middle, None if far_table is None else COARSE.bind(far_table, 0, *rates)


def fetch_kernel(source, target):
    target[...] = source[...]


def relax_kernel(far_ref, fields, near_table, share_ref, arrived_ref):
    fine, middle, _ = bound(fields, near_table)
    position = lax.axis_index("tm")
    first = loaded(fields)
    prior = choose(position == 1, first, loaded(far_ref))
    for _ in range(STEPS_DEV):
        prior = fine(prior)
    shifted = choose(position == 0, first, prior)
    leap = middle(shifted)
    arrived = shifted
    for _ in range(STEPS_DEV):
        arrived = fine(arrived)
    share_ref[...] = merge(choose(position % GROUP == 0, shifted, minus(arrived, leap)))
    arrived_ref[...] = merge(arrived)


def chain(step, load, state, start, count, block):
    single = count % block

    def turn(j, state):
        return step(state, spread(load(j)))

    def turns(t, state):
        for i in range(block):
            state = turn(start + single + t * block + i, state)
        return state

    state = lax.fori_loop(start, start + single, turn, state) if not isinstance(single, int) or single else state
    return lax.fori_loop(0, count // block, turns, state)


def group_kernel(
    shares_ref, near_ref, arrived_ref, fields, near_table, far_table,
    first_ref, rhs_ref, parts_ref, residual_out, residual_ref, sems,
):
    fine, middle, coarse = bound(fields, near_table, far_table)
    position = lax.axis_index("tm")
    own = choose(position == 0, loaded(fields), loaded(near_ref))
    start = spread(shares_ref[0])
    state = start
    for _ in range(STEPS_DEV):
        state, own = fine.two(state, own)
    unpack_to(residual_ref, minus(spread(arrived_ref[...]), own))
    residual_copy = pltpu.make_async_copy(residual_ref, residual_out, sems.at[0])
    residual_copy.start()
    leap, handed = middle(start), coarse(start)
    first_ref[...] = merge(minus(state, leap))
    state = chain(middle, lambda j: shares_ref[j], state, 1, GROUP - 1, 5)
    rhs = merge(choose(position < GROUP, state, minus(state, handed)))
    rhs_ref[...] = rhs
    part = jnp.where(position % 2 == 0, rhs[: GRID // 2], rhs[GRID // 2 :])
    for g in range(parts_ref.shape[0]):
        parts_ref[g] = part
    residual_copy.wait()


def correct_kernel(
    sides_ref, rhs_ref, shares_ref, first_ref, fields, near_table, far_table,
    points_out, value_out, defect_out, points_ref, value_ref, defect_ref, sems,
):
    fine, middle, coarse = bound(fields, near_table, far_table)
    position = lax.axis_index("tm")
    member, group_id = position % GROUP, position // GROUP

    def coarse_side(g):
        return jnp.concatenate([sides_ref[0, g], sides_ref[1, g]], 0)

    steps = jnp.maximum(group_id - 1, 0)
    earlier = chain(coarse, coarse_side, spread(coarse_side(0)), 1, steps, 5)
    earlier = choose(group_id == 0, loaded(fields), earlier)
    own_side = spread(rhs_ref[...])
    value = choose(group_id == 0, own_side, coarse(earlier, own_side))
    copies = []

    def emit(source, target):
        copies.append(pltpu.make_async_copy(source, target, sems.at[len(copies)]))
        copies[-1].start()

    unpack_to(value_ref, value)
    emit(value_ref, value_out.at[0])

    def right_side(j):
        return jnp.where(j == 0, first_ref[...], shares_ref[j])

    prior = chain(middle, right_side, earlier, 0, member, 3)
    side = spread(right_side(member))
    updated = middle(prior, side)
    closing = member == GROUP - 1
    unpack_to(points_ref.at[STEPS_DEV - 1], choose(closing, value, updated))
    emit(points_ref.at[STEPS_DEV - 1], points_out.at[STEPS_DEV - 1])
    unpack_to(defect_ref, choose(closing, minus(updated, value), minus(value, value)))
    emit(defect_ref, defect_out.at[0])
    state = prior
    for i in range(STEPS_DEV - 1):
        state = fine(state)
        unpack_to(points_ref.at[i], state)
        emit(points_ref.at[i], points_out.at[i])
    for copy in copies:
        copy.wait()


VMEM = pl.BlockSpec(memory_space=pltpu.VMEM)
HBM = pl.BlockSpec(memory_space=pltpu.HBM)


def call(kernel, shapes, in_specs, out_specs, scratch, *operands):
    return pl.pallas_call(
        kernel,
        out_shape=[jax.ShapeDtypeStruct(s, jnp.float32) for s in shapes],
        in_specs=in_specs,
        out_specs=out_specs,
        scratch_shapes=scratch,
        compiler_params=pltpu.CompilerParams(vmem_limit_bytes=16 * 2**20),
    )(*operands)


def shards(initial, coarse_guess, feed_rate, kill_rate):
    devices = lax.axis_size("tm")
    groups = devices // GROUP
    field, pair, half = (GRID, LANES), (2, GRID, GRID), (GRID // 2, LANES)
    own = coarse_guess[0]
    far = lax.ppermute(own, "tm", [(i, i + 2) for i in range(devices - 2)])
    far_table = jnp.asarray(COARSE.tables)
    fields = jnp.concatenate([initial, feed_rate[None], kill_rate[None]], 0)
    near_table = pl.pallas_call(
        fetch_kernel,
        out_shape=jax.ShapeDtypeStruct(near_tables.shape, jnp.bfloat16),
        in_specs=[VMEM],
        out_specs=VMEM,
        cost_estimate=pl.CostEstimate(flops=0, bytes_accessed=4 * near_tables.size, transcendentals=0),
        compiler_params=pltpu.CompilerParams(vmem_limit_bytes=16 * 2**20),
    )(jnp.asarray(near_tables))
    near_table, own = lax.optimization_barrier((near_table, own))
    near = lax.ppermute(own, "tm", [(i, i + 1) for i in range(devices - 1)])
    share, arrived = call(relax_kernel, [field] * 2, [VMEM] * 3, [VMEM] * 2, [], far, fields, near_table)
    inside = [[g * GROUP + m for m in range(GROUP)] for g in range(groups)]
    shares = lax.all_gather(share, "tm", axis_index_groups=inside)
    parts_shape = (groups,) + half
    first, rhs, parts, residual = call(
        group_kernel,
        [field, field, parts_shape, pair],
        [VMEM] * 6,
        [VMEM] * 3 + [HBM],
        [pltpu.VMEM(pair, jnp.float32), pltpu.SemaphoreType.DMA((1,))],
        shares, near, arrived, fields, near_table, far_table,
    )
    across = [[g * GROUP + m for g in range(groups)] for m in range(GROUP)]
    parts = lax.all_to_all(parts, "tm", 0, 0, axis_index_groups=across)
    cores = [[2 * c, 2 * c + 1] for c in range(devices // 2)]
    sides = lax.all_gather(parts[: groups - 1], "tm", axis_index_groups=cores)
    shapes = [(STEPS_DEV,) + pair, pair, pair]
    points, value, defect = call(
        correct_kernel,
        [(STEPS_DEV,) + pair, (1,) + pair, (1,) + pair],
        [VMEM] * 7,
        [HBM] * 3,
        [pltpu.VMEM(s, jnp.float32) for s in shapes] + [pltpu.SemaphoreType.DMA((STEPS_DEV + 2,))],
        sides, rhs, shares, first, fields, near_table, far_table,
    )
    return points, residual[None], value, defect


def solution(mesh):
    in_specs = (P(), P("tm", None, None, None), P(), P())
    out_specs = (P("tm", None, None, None),) * 4
    return jax.shard_map(shards, mesh=mesh, in_specs=in_specs, out_specs=out_specs, check_vma=False)
```

```python
import functools

import jax
import jax.numpy as jnp
import ml_dtypes
import numpy as np
from jax import lax
from jax.experimental import pallas as pl
from jax.experimental.pallas import tpu as pltpu
from jax.sharding import PartitionSpec as P

GRID = 64
GROUP = 16
STEPS_DEV = 4
LANES = 2 * GRID
diffusion = (0.2, 0.1)
interval_time = 0.03125
fine_step = interval_time / STEPS_DEV
level_step = interval_time
coarse_step = interval_time * GROUP


def basis_tables():
    positions = np.arange(GRID, dtype=np.float32)
    angles = np.float32(np.pi) * (positions[:, None] + np.float32(0.5)) * positions[None] / np.float32(GRID)
    weight = np.where(positions == 0, np.sqrt(np.float32(1 / GRID)), np.sqrt(np.float32(2 / GRID)))
    cosines = np.cos(angles.astype(np.float64)).astype(np.float32)
    basis = cosines * weight[None].astype(np.float32)
    sines = np.sin((np.float32(np.pi) * positions / np.float32(2 * GRID)).astype(np.float64)).astype(np.float32)
    return basis.astype(np.float64), (np.float32(-4) * sines * sines).astype(np.float64)


def solve_terms(time_step, rate, rank):
    basis, values = basis_tables()
    inverse = 1 / (1 - time_step * rate * (values[:, None] + values[None]))
    side = inverse[:, 0] - 1
    rest = inverse - 1 - side[:, None] - side[None]
    weights, vectors = np.linalg.eigh(rest)
    order = np.argsort(-np.abs(weights))[:rank]
    first = (basis * side) @ basis.T + basis @ basis.T - np.eye(GRID)
    cross = [(basis * (vectors[:, k] * np.sqrt(np.abs(weights[k])))) @ basis.T for k in order]
    return first, cross, [np.sign(weights[k]) for k in order]


def halves(matrix):
    high = matrix.astype(np.float32).astype(ml_dtypes.bfloat16)
    low = (matrix - high.astype(np.float64)).astype(np.float32).astype(ml_dtypes.bfloat16)
    return high, low


def twice(matrix):
    return np.concatenate([matrix, matrix], 1)


def species_tables(time_step, rate, rank, fine_cross):
    first, cross, signs = solve_terms(time_step, rate, rank)
    high, low = halves(first)
    right = np.concatenate([twice(high), twice(low), twice(high), np.zeros_like(twice(low))], 0)
    left = [high, high, low]
    cross_high, cross_low = zip(*[halves(m) for m in cross])
    cross_high = np.concatenate([twice(m) for m in cross_high], 1)
    cross_low = np.concatenate([twice(m) for m in cross_low], 1)
    parts = [cross_high, cross_low, cross_high] if fine_cross else [cross_high, cross_low]
    blank = np.zeros((4 * GRID - GRID * len(parts), cross_high.shape[1]), ml_dtypes.bfloat16)
    mixing = np.concatenate(parts + [blank], 0)
    for k, (matrix, sign) in enumerate(zip(cross, signs)):
        high, low = halves(matrix * sign)
        left += [high, high, low] if k < fine_cross else [high]
    return right, mixing, np.concatenate(left, 1)


@functools.lru_cache(None)
def level_tables(time_step, rank, fine_cross):
    sub = species_tables(time_step, diffusion[0], rank, fine_cross)
    cat = species_tables(time_step, diffusion[1], rank, fine_cross)
    left = np.concatenate([sub[2], cat[2]], 0)
    left = np.concatenate([left, np.zeros_like(left)], 0)
    return np.concatenate([sub[0], sub[1], cat[0], cat[1], left], 1)


def product(left, right):
    return jnp.dot(left, right, preferred_element_type=jnp.float32)


def second_half():
    return lax.broadcasted_iota(jnp.int32, (GRID, LANES), 1) >= GRID


def spread(fields):
    turned = pltpu.roll(fields, GRID, 1)
    second = second_half()
    return jnp.where(second, turned, fields), jnp.where(second, fields, turned)


def merge(state):
    return jnp.where(second_half(), state[1], state[0])


def loaded(pair):
    return tuple(jnp.concatenate([pair[i], pair[i]], 1) for i in range(2))


def unpack_to(ref, state):
    ref[0] = state[0][:, :GRID]
    ref[1] = state[1][:, :GRID]


def choose(condition, one, other):
    return tuple(jnp.where(condition, a, b) for a, b in zip(one, other))


def plus(one, other):
    return tuple(a + b for a, b in zip(one, other))


def minus(one, other):
    return tuple(a - b for a, b in zip(one, other))


class Level:
    def __init__(self, time_step, rank, fine_cross):
        self.time_step, self.rank, self.fine_cross = time_step, rank, fine_cross
        self.tables = level_tables(time_step, rank, fine_cross)
        self.width = self.tables.shape[1]

    def bind(self, table, start, feed, kill):
        h = jnp.float32(self.time_step)
        rank, fine_cross = self.rank, self.fine_cross
        cross = LANES * rank
        supply, decay = h * feed, h * (feed + kill)
        wide_at = [start, start + LANES + cross]
        left_at = start + 2 * (LANES + cross)

        def solve(values):
            count = values[0].shape[0] // GRID
            rows = [slice(GRID * n, GRID * (n + 1)) for n in range(count)]
            made = []
            for i, value in enumerate(values):
                high = value.astype(jnp.bfloat16)
                rest = (value - high.astype(jnp.float32)).astype(jnp.bfloat16)
                wide = jnp.concatenate([high, rest], 1)
                at, stop = wide_at[i], wide_at[i] + LANES + cross
                if fine_cross:
                    right = product(wide, table[:, at:stop])
                    right, turned = right[:, :LANES], right[:, LANES:]
                else:
                    turned = product(high, table[: 2 * GRID, at + LANES : stop])
                    right = None
                made.append((high, rest, wide, turned, right))
            solved = []
            for i, (high, rest, wide, turned, right) in enumerate(made):
                if not fine_cross:
                    right = product(wide, table[:, wide_at[i] : wide_at[i] + LANES])
                stack = [high, rest, high]
                for k in range(rank):
                    part = turned[:, LANES * k : LANES * (k + 1)]
                    part_high = part.astype(jnp.bfloat16)
                    stack.append(part_high)
                    if k < fine_cross:
                        stack += [(part - part_high.astype(jnp.float32)).astype(jnp.bfloat16), part_high]
                stack = jnp.concatenate([jnp.concatenate([p[r] for p in stack], 0) for r in rows], 1)
                left = product(table[GRID * i : GRID * (i + 1), left_at : left_at + stack.shape[0]], stack)
                left = jnp.concatenate([left[:, LANES * n : LANES * (n + 1)] for n in range(count)], 0)
                solved.append((right, left))
            return solved

        def react(state):
            sub, cat = state
            uptake = (h * sub) * (cat * cat)
            return sub + (supply - supply * sub - uptake), cat + (uptake - decay * cat)

        def step(state, extra=None):
            values = react(state)
            sums = [a + b for a, b in solve(values)]
            if extra is not None:
                sums = [a + b for a, b in zip(sums, extra)]
            return tuple(a + b for a, b in zip(values, sums))

        def step_two(one, other):
            values = [jnp.concatenate(pair, 0) for pair in zip(react(one), react(other))]
            values = [a + (b + c) for a, (b, c) in zip(values, solve(values))]
            return tuple(v[:GRID] for v in values), tuple(v[GRID:] for v in values)

        step.two = step_two
        return step


FINE = Level(fine_step, 1, 0)
MIDDLE = Level(level_step, 1, 1)
COARSE = Level(coarse_step, 3, 1)
near_tables = np.concatenate([FINE.tables, MIDDLE.tables], 1)


def bound(fields, near_table, far_table=None):
    rates = loaded(fields.at[2:4])
    fine, middle = FINE.bind(near_table, 0, *rates), MIDDLE.bind(near_table, FINE.width, *rates)
    return fine, middle, None if far_table is None else COARSE.bind(far_table, 0, *rates)


def fetch_kernel(source, target):
    target[...] = source[...]


def relax_kernel(far_ref, fields, near_table, share_ref, arrived_ref):
    fine, middle, _ = bound(fields, near_table)
    position = lax.axis_index("tm")
    first = loaded(fields)
    prior = choose(position == 1, first, loaded(far_ref))
    for _ in range(STEPS_DEV):
        prior = fine(prior)
    shifted = choose(position == 0, first, prior)
    leap = middle(shifted)
    arrived = shifted
    for _ in range(STEPS_DEV):
        arrived = fine(arrived)
    share_ref[...] = merge(choose(position % GROUP == 0, shifted, minus(arrived, leap)))
    arrived_ref[...] = merge(arrived)


def chain(step, load, state, start, count, block):
    single = count % block

    def turn(j, state):
        return step(state, spread(load(j)))

    def turns(t, state):
        for i in range(block):
            state = turn(start + single + t * block + i, state)
        return state

    state = lax.fori_loop(start, start + single, turn, state) if not isinstance(single, int) or single else state
    return lax.fori_loop(0, count // block, turns, state)


def group_kernel(
    shares_ref, near_ref, arrived_ref, fields, near_table, far_table,
    first_ref, rhs_ref, parts_ref, residual_out, residual_ref, sems,
):
    fine, middle, coarse = bound(fields, near_table, far_table)
    position = lax.axis_index("tm")
    own = choose(position == 0, loaded(fields), loaded(near_ref))
    start = spread(shares_ref[0])
    state = start
    for _ in range(STEPS_DEV):
        state, own = fine.two(state, own)
    unpack_to(residual_ref, minus(spread(arrived_ref[...]), own))
    residual_copy = pltpu.make_async_copy(residual_ref, residual_out, sems.at[0])
    residual_copy.start()
    leap, handed = middle(start), coarse(start)
    first_ref[...] = merge(minus(state, leap))
    state = chain(middle, lambda j: shares_ref[j], state, 1, GROUP - 1, 5)
    rhs = merge(choose(position < GROUP, state, minus(state, handed)))
    rhs_ref[...] = rhs
    part = jnp.where(position % 2 == 0, rhs[: GRID // 2], rhs[GRID // 2 :])
    for g in range(parts_ref.shape[0]):
        parts_ref[g] = part
    residual_copy.wait()


def correct_kernel(
    sides_ref, rhs_ref, shares_ref, first_ref, fields, near_table, far_table,
    points_out, value_out, defect_out, points_ref, value_ref, defect_ref, sems,
):
    fine, middle, coarse = bound(fields, near_table, far_table)
    position = lax.axis_index("tm")
    member, group_id = position % GROUP, position // GROUP

    def coarse_side(g):
        return jnp.concatenate([sides_ref[0, g], sides_ref[1, g]], 0)

    steps = jnp.maximum(group_id - 1, 0)
    earlier = chain(coarse, coarse_side, spread(coarse_side(0)), 1, steps, 10)
    earlier = choose(group_id == 0, loaded(fields), earlier)
    copies = []

    def emit(source, target):
        copies.append(pltpu.make_async_copy(source, target, sems.at[len(copies)]))
        copies[-1].start()

    def right_side(j):
        return jnp.where(j == 0, first_ref[...], shares_ref[j])

    prior = chain(middle, right_side, earlier, 0, member, 3)
    updated = middle(prior, spread(right_side(member)))
    own_side = spread(rhs_ref[...])
    value = choose(group_id == 0, own_side, coarse(earlier, own_side))
    closing = member == GROUP - 1
    state = prior
    for i in range(STEPS_DEV - 1):
        state = fine(state)
        unpack_to(points_ref.at[i], state)
        emit(points_ref.at[i], points_out.at[i])
        if i == 0:
            unpack_to(value_ref, value)
            emit(value_ref, value_out.at[0])
            unpack_to(points_ref.at[STEPS_DEV - 1], choose(closing, value, updated))
            emit(points_ref.at[STEPS_DEV - 1], points_out.at[STEPS_DEV - 1])
            unpack_to(defect_ref, choose(closing, minus(updated, value), minus(value, value)))
            emit(defect_ref, defect_out.at[0])
    for copy in copies:
        copy.wait()


VMEM = pl.BlockSpec(memory_space=pltpu.VMEM)
HBM = pl.BlockSpec(memory_space=pltpu.HBM)


def call(kernel, shapes, in_specs, out_specs, scratch, *operands):
    return pl.pallas_call(
        kernel,
        out_shape=[jax.ShapeDtypeStruct(s, jnp.float32) for s in shapes],
        in_specs=in_specs,
        out_specs=out_specs,
        scratch_shapes=scratch,
        compiler_params=pltpu.CompilerParams(vmem_limit_bytes=16 * 2**20),
    )(*operands)


def shards(initial, coarse_guess, feed_rate, kill_rate):
    devices = lax.axis_size("tm")
    groups = devices // GROUP
    field, pair, half = (GRID, LANES), (2, GRID, GRID), (GRID // 2, LANES)
    own = coarse_guess[0]
    far = lax.ppermute(own, "tm", [(i, i + 2) for i in range(devices - 2)])
    far_table = jnp.asarray(COARSE.tables)
    fields = jnp.concatenate([initial, feed_rate[None], kill_rate[None]], 0)
    near_table = pl.pallas_call(
        fetch_kernel,
        out_shape=jax.ShapeDtypeStruct(near_tables.shape, jnp.bfloat16),
        in_specs=[VMEM],
        out_specs=VMEM,
        cost_estimate=pl.CostEstimate(flops=0, bytes_accessed=4 * near_tables.size, transcendentals=0),
        compiler_params=pltpu.CompilerParams(vmem_limit_bytes=16 * 2**20),
    )(jnp.asarray(near_tables))
    near_table, own = lax.optimization_barrier((near_table, own))
    near = lax.ppermute(own, "tm", [(i, i + 1) for i in range(devices - 1)])
    share, arrived = call(relax_kernel, [field] * 2, [VMEM] * 3, [VMEM] * 2, [], far, fields, near_table)
    inside = [[g * GROUP + m for m in range(GROUP)] for g in range(groups)]
    shares = lax.all_gather(share, "tm", axis_index_groups=inside)
    parts_shape = (groups,) + half
    first, rhs, parts, residual = call(
        group_kernel,
        [field, field, parts_shape, pair],
        [VMEM] * 6,
        [VMEM] * 3 + [HBM],
        [pltpu.VMEM(pair, jnp.float32), pltpu.SemaphoreType.DMA((1,))],
        shares, near, arrived, fields, near_table, far_table,
    )
    across = [[g * GROUP + m for g in range(groups)] for m in range(GROUP)]
    parts = lax.all_to_all(parts, "tm", 0, 0, axis_index_groups=across)
    cores = [[2 * c, 2 * c + 1] for c in range(devices // 2)]
    sides = lax.all_gather(parts[: groups - 1], "tm", axis_index_groups=cores)
    shapes = [(STEPS_DEV,) + pair, pair, pair]
    points, value, defect = call(
        correct_kernel,
        [(STEPS_DEV,) + pair, (1,) + pair, (1,) + pair],
        [VMEM] * 7,
        [HBM] * 3,
        [pltpu.VMEM(s, jnp.float32) for s in shapes] + [pltpu.SemaphoreType.DMA((STEPS_DEV + 2,))],
        sides, rhs, shares, first, fields, near_table, far_table,
    )
    return points, residual[None], value, defect


def solution(mesh):
    in_specs = (P(), P("tm", None, None, None), P(), P())
    out_specs = (P("tm", None, None, None),) * 4
    return jax.shard_map(shards, mesh=mesh, in_specs=in_specs, out_specs=out_specs, check_vma=False)
```

```python
import functools

import jax
import jax.numpy as jnp
import ml_dtypes
import numpy as np
from jax import lax
from jax.experimental import pallas as pl
from jax.experimental.pallas import tpu as pltpu
from jax.sharding import PartitionSpec as P

GRID = 64
GROUP = 16
STEPS_DEV = 4
LANES = 2 * GRID
diffusion = (0.2, 0.1)
interval_time = 0.03125
fine_step = interval_time / STEPS_DEV
level_step = interval_time
coarse_step = interval_time * GROUP


def basis_tables():
    positions = np.arange(GRID, dtype=np.float32)
    angles = np.float32(np.pi) * (positions[:, None] + np.float32(0.5)) * positions[None] / np.float32(GRID)
    weight = np.where(positions == 0, np.sqrt(np.float32(1 / GRID)), np.sqrt(np.float32(2 / GRID)))
    cosines = np.cos(angles.astype(np.float64)).astype(np.float32)
    basis = cosines * weight[None].astype(np.float32)
    sines = np.sin((np.float32(np.pi) * positions / np.float32(2 * GRID)).astype(np.float64)).astype(np.float32)
    return basis.astype(np.float64), (np.float32(-4) * sines * sines).astype(np.float64)


def solve_terms(time_step, rate, rank):
    basis, values = basis_tables()
    inverse = 1 / (1 - time_step * rate * (values[:, None] + values[None]))
    side = inverse[:, 0] - 1
    rest = inverse - 1 - side[:, None] - side[None]
    weights, vectors = np.linalg.eigh(rest)
    order = np.argsort(-np.abs(weights))[:rank]
    first = (basis * side) @ basis.T + basis @ basis.T - np.eye(GRID)
    cross = [(basis * (vectors[:, k] * np.sqrt(np.abs(weights[k])))) @ basis.T for k in order]
    return first, cross, [np.sign(weights[k]) for k in order]


def halves(matrix):
    high = matrix.astype(np.float32).astype(ml_dtypes.bfloat16)
    low = (matrix - high.astype(np.float64)).astype(np.float32).astype(ml_dtypes.bfloat16)
    return high, low


def twice(matrix):
    return np.concatenate([matrix, matrix], 1)


def species_tables(time_step, rate, rank, fine_cross):
    first, cross, signs = solve_terms(time_step, rate, rank)
    high, low = halves(first)
    right = np.concatenate([twice(high), twice(low), twice(high), np.zeros_like(twice(low))], 0)
    left = [high, high, low]
    cross_high, cross_low = zip(*[halves(m) for m in cross])
    cross_high = np.concatenate([twice(m) for m in cross_high], 1)
    cross_low = np.concatenate([twice(m) for m in cross_low], 1)
    parts = [cross_high, cross_low, cross_high] if fine_cross else [cross_high, cross_low]
    blank = np.zeros((4 * GRID - GRID * len(parts), cross_high.shape[1]), ml_dtypes.bfloat16)
    mixing = np.concatenate(parts + [blank], 0)
    for k, (matrix, sign) in enumerate(zip(cross, signs)):
        high, low = halves(matrix * sign)
        left += [high, high, low] if k < fine_cross else [high]
    return right, mixing, np.concatenate(left, 1)


@functools.lru_cache(None)
def level_tables(time_step, rank, fine_cross):
    sub = species_tables(time_step, diffusion[0], rank, fine_cross)
    cat = species_tables(time_step, diffusion[1], rank, fine_cross)
    left = np.concatenate([sub[2], cat[2]], 0)
    left = np.concatenate([left, np.zeros_like(left)], 0)
    return np.concatenate([sub[0], sub[1], cat[0], cat[1], left], 1)


def product(left, right):
    return jnp.dot(left, right, preferred_element_type=jnp.float32)


def second_half():
    return lax.broadcasted_iota(jnp.int32, (GRID, LANES), 1) >= GRID


def spread(fields):
    turned = pltpu.roll(fields, GRID, 1)
    second = second_half()
    return jnp.where(second, turned, fields), jnp.where(second, fields, turned)


def merge(state):
    return jnp.where(second_half(), state[1], state[0])


def loaded(pair):
    return tuple(jnp.concatenate([pair[i], pair[i]], 1) for i in range(2))


def unpack_to(ref, state):
    ref[0] = state[0][:, :GRID]
    ref[1] = state[1][:, :GRID]


def choose(condition, one, other):
    return tuple(jnp.where(condition, a, b) for a, b in zip(one, other))


def plus(one, other):
    return tuple(a + b for a, b in zip(one, other))


def minus(one, other):
    return tuple(a - b for a, b in zip(one, other))


class Level:
    def __init__(self, time_step, rank, fine_cross):
        self.time_step, self.rank, self.fine_cross = time_step, rank, fine_cross
        self.tables = level_tables(time_step, rank, fine_cross)
        self.width = self.tables.shape[1]

    def bind(self, table, start, feed, kill):
        h = jnp.float32(self.time_step)
        rank, fine_cross = self.rank, self.fine_cross
        cross = LANES * rank
        supply, decay = h * feed, h * (feed + kill)
        wide_at = [start, start + LANES + cross]
        left_at = start + 2 * (LANES + cross)

        def solve(values):
            count = values[0].shape[0] // GRID
            rows = [slice(GRID * n, GRID * (n + 1)) for n in range(count)]
            made = []
            for i, value in enumerate(values):
                high = value.astype(jnp.bfloat16)
                rest = (value - high.astype(jnp.float32)).astype(jnp.bfloat16)
                wide = jnp.concatenate([high, rest], 1)
                at, stop = wide_at[i], wide_at[i] + LANES + cross
                if fine_cross:
                    right = product(wide, table[:, at:stop])
                    right, turned = right[:, :LANES], right[:, LANES:]
                else:
                    turned = product(high, table[: 2 * GRID, at + LANES : stop])
                    right = None
                made.append((high, rest, wide, turned, right))
            solved = []
            for i, (high, rest, wide, turned, right) in enumerate(made):
                if not fine_cross:
                    right = product(wide, table[:, wide_at[i] : wide_at[i] + LANES])
                stack = [high, rest, high]
                for k in range(rank):
                    part = turned[:, LANES * k : LANES * (k + 1)]
                    part_high = part.astype(jnp.bfloat16)
                    stack.append(part_high)
                    if k < fine_cross:
                        stack += [(part - part_high.astype(jnp.float32)).astype(jnp.bfloat16), part_high]
                stack = jnp.concatenate([jnp.concatenate([p[r] for p in stack], 0) for r in rows], 1)
                left = product(table[GRID * i : GRID * (i + 1), left_at : left_at + stack.shape[0]], stack)
                left = jnp.concatenate([left[:, LANES * n : LANES * (n + 1)] for n in range(count)], 0)
                solved.append((right, left))
            return solved

        def react(state):
            sub, cat = state
            uptake = (h * sub) * (cat * cat)
            return sub + (supply - supply * sub - uptake), cat + (uptake - decay * cat)

        def step(state, extra=None):
            values = react(state)
            solved = solve(values)
            if extra is not None:
                values = plus(values, extra)
            return tuple((value + right) + left for value, (right, left) in zip(values, solved))

        def step_two(one, other):
            values = [jnp.concatenate(pair, 0) for pair in zip(react(one), react(other))]
            values = [(a + b) + c for a, (b, c) in zip(values, solve(values))]
            return tuple(v[:GRID] for v in values), tuple(v[GRID:] for v in values)

        step.two = step_two
        return step


FINE = Level(fine_step, 1, 0)
MIDDLE = Level(level_step, 1, 1)
COARSE = Level(coarse_step, 3, 1)
near_tables = np.concatenate([FINE.tables, MIDDLE.tables], 1)


def bound(fields, near_table, far_table=None):
    rates = loaded(fields.at[2:4])
    fine, middle = FINE.bind(near_table, 0, *rates), MIDDLE.bind(near_table, FINE.width, *rates)
    return fine, middle, None if far_table is None else COARSE.bind(far_table, 0, *rates)


def fetch_kernel(source, target):
    target[...] = source[...]


def relax_kernel(far_ref, fields, near_table, share_ref, arrived_ref):
    fine, middle, _ = bound(fields, near_table)
    position = lax.axis_index("tm")
    first = loaded(fields)
    prior = choose(position == 1, first, loaded(far_ref))
    for _ in range(STEPS_DEV):
        prior = fine(prior)
    shifted = choose(position == 0, first, prior)
    leap = middle(shifted)
    arrived = shifted
    for _ in range(STEPS_DEV):
        arrived = fine(arrived)
    share_ref[...] = merge(choose(position % GROUP == 0, shifted, minus(arrived, leap)))
    arrived_ref[...] = merge(arrived)


def chain(step, load, state, start, count, block):
    single = count % block

    def turn(j, state):
        return step(state, spread(load(j)))

    def turns(t, state):
        for i in range(block):
            state = turn(start + single + t * block + i, state)
        return state

    state = lax.fori_loop(start, start + single, turn, state) if not isinstance(single, int) or single else state
    return lax.fori_loop(0, count // block, turns, state)


def group_kernel(
    shares_ref, near_ref, arrived_ref, fields, near_table, far_table,
    first_ref, rhs_ref, parts_ref, residual_out, residual_ref, sems,
):
    fine, middle, coarse = bound(fields, near_table, far_table)
    position = lax.axis_index("tm")
    own = choose(position == 0, loaded(fields), loaded(near_ref))
    start = spread(shares_ref[0])
    state = start
    for _ in range(STEPS_DEV):
        state, own = fine.two(state, own)
    unpack_to(residual_ref, minus(spread(arrived_ref[...]), own))
    residual_copy = pltpu.make_async_copy(residual_ref, residual_out, sems.at[0])
    residual_copy.start()
    leap, handed = middle(start), coarse(start)
    first_ref[...] = merge(minus(state, leap))
    state = chain(middle, lambda j: shares_ref[j], state, 1, GROUP - 1, GROUP - 1)
    rhs = merge(choose(position < GROUP, state, minus(state, handed)))
    rhs_ref[...] = rhs
    part = jnp.where(position % 2 == 0, rhs[: GRID // 2], rhs[GRID // 2 :])
    for g in range(parts_ref.shape[0]):
        parts_ref[g] = part
    residual_copy.wait()


def correct_kernel(
    sides_ref, rhs_ref, shares_ref, first_ref, fields, near_table, far_table,
    points_out, value_out, defect_out, points_ref, value_ref, defect_ref, sems,
):
    fine, middle, coarse = bound(fields, near_table, far_table)
    position = lax.axis_index("tm")
    member, group_id = position % GROUP, position // GROUP

    def coarse_side(g):
        return jnp.concatenate([sides_ref[0, g], sides_ref[1, g]], 0)

    steps = jnp.maximum(group_id - 1, 0)
    earlier = chain(coarse, coarse_side, spread(coarse_side(0)), 1, steps, 10)
    earlier = choose(group_id == 0, loaded(fields), earlier)
    copies = []

    def emit(source, target):
        copies.append(pltpu.make_async_copy(source, target, sems.at[len(copies)]))
        copies[-1].start()

    def right_side(j):
        return jnp.where(j == 0, first_ref[...], shares_ref[j])

    prior = chain(middle, right_side, earlier, 0, member, 3)
    updated = middle(prior, spread(right_side(member)))
    own_side = spread(rhs_ref[...])
    value = choose(group_id == 0, own_side, coarse(earlier, own_side))
    closing = member == GROUP - 1
    state = prior
    for i in range(STEPS_DEV - 1):
        state = fine(state)
        unpack_to(points_ref.at[i], state)
        emit(points_ref.at[i], points_out.at[i])
        if i == 0:
            unpack_to(value_ref, value)
            emit(value_ref, value_out.at[0])
            unpack_to(points_ref.at[STEPS_DEV - 1], choose(closing, value, updated))
            emit(points_ref.at[STEPS_DEV - 1], points_out.at[STEPS_DEV - 1])
            unpack_to(defect_ref, choose(closing, minus(updated, value), minus(value, value)))
            emit(defect_ref, defect_out.at[0])
    for copy in copies:
        copy.wait()


VMEM = pl.BlockSpec(memory_space=pltpu.VMEM)
HBM = pl.BlockSpec(memory_space=pltpu.HBM)


def call(kernel, shapes, in_specs, out_specs, scratch, *operands):
    return pl.pallas_call(
        kernel,
        out_shape=[jax.ShapeDtypeStruct(s, jnp.float32) for s in shapes],
        in_specs=in_specs,
        out_specs=out_specs,
        scratch_shapes=scratch,
        compiler_params=pltpu.CompilerParams(vmem_limit_bytes=16 * 2**20),
    )(*operands)


def shards(initial, coarse_guess, feed_rate, kill_rate):
    devices = lax.axis_size("tm")
    groups = devices // GROUP
    field, pair, half = (GRID, LANES), (2, GRID, GRID), (GRID // 2, LANES)
    own = coarse_guess[0]
    far = lax.ppermute(own, "tm", [(i, i + 2) for i in range(devices - 2)])
    far_table = jnp.asarray(COARSE.tables)
    fields = jnp.concatenate([initial, feed_rate[None], kill_rate[None]], 0)
    near_table = pl.pallas_call(
        fetch_kernel,
        out_shape=jax.ShapeDtypeStruct(near_tables.shape, jnp.bfloat16),
        in_specs=[VMEM],
        out_specs=VMEM,
        cost_estimate=pl.CostEstimate(flops=0, bytes_accessed=4 * near_tables.size, transcendentals=0),
        compiler_params=pltpu.CompilerParams(vmem_limit_bytes=16 * 2**20),
    )(jnp.asarray(near_tables))
    near_table, own = lax.optimization_barrier((near_table, own))
    near = lax.ppermute(own, "tm", [(i, i + 1) for i in range(devices - 1)])
    share, arrived = call(relax_kernel, [field] * 2, [VMEM] * 3, [VMEM] * 2, [], far, fields, near_table)
    inside = [[g * GROUP + m for m in range(GROUP)] for g in range(groups)]
    shares = lax.all_gather(share, "tm", axis_index_groups=inside)
    parts_shape = (groups,) + half
    first, rhs, parts, residual = call(
        group_kernel,
        [field, field, parts_shape, pair],
        [VMEM] * 6,
        [VMEM] * 3 + [HBM],
        [pltpu.VMEM(pair, jnp.float32), pltpu.SemaphoreType.DMA((1,))],
        shares, near, arrived, fields, near_table, far_table,
    )
    across = [[g * GROUP + m for g in range(groups)] for m in range(GROUP)]
    parts = lax.all_to_all(parts, "tm", 0, 0, axis_index_groups=across)
    cores = [[2 * c, 2 * c + 1] for c in range(devices // 2)]
    sides = lax.all_gather(parts[: groups - 1], "tm", axis_index_groups=cores)
    shapes = [(STEPS_DEV,) + pair, pair, pair]
    points, value, defect = call(
        correct_kernel,
        [(STEPS_DEV,) + pair, (1,) + pair, (1,) + pair],
        [VMEM] * 7,
        [HBM] * 3,
        [pltpu.VMEM(s, jnp.float32) for s in shapes] + [pltpu.SemaphoreType.DMA((STEPS_DEV + 2,))],
        sides, rhs, shares, first, fields, near_table, far_table,
    )
    return points, residual[None], value, defect


def solution(mesh):
    in_specs = (P(), P("tm", None, None, None), P(), P())
    out_specs = (P("tm", None, None, None),) * 4
    return jax.shard_map(shards, mesh=mesh, in_specs=in_specs, out_specs=out_specs, check_vma=False)
```

```python
import functools

import jax
import jax.numpy as jnp
import ml_dtypes
import numpy as np
from jax import lax
from jax.experimental import pallas as pl
from jax.experimental.pallas import tpu as pltpu
from jax.sharding import PartitionSpec as P

GRID = 64
GROUP = 16
STEPS_DEV = 4
LANES = 2 * GRID
diffusion = (0.2, 0.1)
interval_time = 0.03125
fine_step = interval_time / STEPS_DEV
level_step = interval_time
coarse_step = interval_time * GROUP


def basis_tables():
    positions = np.arange(GRID, dtype=np.float32)
    angles = np.float32(np.pi) * (positions[:, None] + np.float32(0.5)) * positions[None] / np.float32(GRID)
    weight = np.where(positions == 0, np.sqrt(np.float32(1 / GRID)), np.sqrt(np.float32(2 / GRID)))
    cosines = np.cos(angles.astype(np.float64)).astype(np.float32)
    basis = cosines * weight[None].astype(np.float32)
    sines = np.sin((np.float32(np.pi) * positions / np.float32(2 * GRID)).astype(np.float64)).astype(np.float32)
    return basis.astype(np.float64), (np.float32(-4) * sines * sines).astype(np.float64)


def solve_terms(time_step, rate, rank):
    basis, values = basis_tables()
    inverse = 1 / (1 - time_step * rate * (values[:, None] + values[None]))
    side = inverse[:, 0] - 1
    rest = inverse - 1 - side[:, None] - side[None]
    weights, vectors = np.linalg.eigh(rest)
    order = np.argsort(-np.abs(weights))[:rank]
    first = (basis * side) @ basis.T + basis @ basis.T - np.eye(GRID)
    cross = [(basis * (vectors[:, k] * np.sqrt(np.abs(weights[k])))) @ basis.T for k in order]
    return first, cross, [np.sign(weights[k]) for k in order]


def halves(matrix):
    high = matrix.astype(np.float32).astype(ml_dtypes.bfloat16)
    low = (matrix - high.astype(np.float64)).astype(np.float32).astype(ml_dtypes.bfloat16)
    return high, low


def twice(matrix):
    return np.concatenate([matrix, matrix], 1)


def species_tables(time_step, rate, rank, fine_cross):
    first, cross, signs = solve_terms(time_step, rate, rank)
    high, low = halves(first)
    right = np.concatenate([twice(high), twice(low), twice(high), np.zeros_like(twice(low))], 0)
    left = [high, high, low]
    cross_high, cross_low = zip(*[halves(m) for m in cross])
    cross_high = np.concatenate([twice(m) for m in cross_high], 1)
    cross_low = np.concatenate([twice(m) for m in cross_low], 1)
    parts = [cross_high, cross_low, cross_high] if fine_cross else [cross_high, cross_low]
    blank = np.zeros((4 * GRID - GRID * len(parts), cross_high.shape[1]), ml_dtypes.bfloat16)
    mixing = np.concatenate(parts + [blank], 0)
    for k, (matrix, sign) in enumerate(zip(cross, signs)):
        high, low = halves(matrix * sign)
        left += [high, high, low] if k < fine_cross else [high]
    return right, mixing, np.concatenate(left, 1)


@functools.lru_cache(None)
def level_tables(time_step, rank, fine_cross):
    sub = species_tables(time_step, diffusion[0], rank, fine_cross)
    cat = species_tables(time_step, diffusion[1], rank, fine_cross)
    left = np.concatenate([sub[2], cat[2]], 0)
    left = np.concatenate([left, np.zeros_like(left)], 0)
    return np.concatenate([sub[0], sub[1], cat[0], cat[1], left], 1)


def product(left, right):
    return jnp.dot(left, right, preferred_element_type=jnp.float32)


def second_half():
    return lax.broadcasted_iota(jnp.int32, (GRID, LANES), 1) >= GRID


def spread(fields):
    turned = pltpu.roll(fields, GRID, 1)
    second = second_half()
    return jnp.where(second, turned, fields), jnp.where(second, fields, turned)


def merge(state):
    return jnp.where(second_half(), state[1], state[0])


def loaded(pair):
    return tuple(jnp.concatenate([pair[i], pair[i]], 1) for i in range(2))


def unpack_to(ref, state):
    ref[0] = state[0][:, :GRID]
    ref[1] = state[1][:, :GRID]


def choose(condition, one, other):
    return tuple(jnp.where(condition, a, b) for a, b in zip(one, other))


def plus(one, other):
    return tuple(a + b for a, b in zip(one, other))


def minus(one, other):
    return tuple(a - b for a, b in zip(one, other))


class Level:
    def __init__(self, time_step, rank, fine_cross):
        self.time_step, self.rank, self.fine_cross = time_step, rank, fine_cross
        self.tables = level_tables(time_step, rank, fine_cross)
        self.width = self.tables.shape[1]

    def bind(self, table, start, feed, kill):
        h = jnp.float32(self.time_step)
        rank, fine_cross = self.rank, self.fine_cross
        cross = LANES * rank
        supply, decay = h * feed, h * (feed + kill)
        wide_at = [start, start + LANES + cross]
        left_at = start + 2 * (LANES + cross)

        def solve(values):
            count = values[0].shape[0] // GRID
            rows = [slice(GRID * n, GRID * (n + 1)) for n in range(count)]
            made = []
            for i, value in enumerate(values):
                high = value.astype(jnp.bfloat16)
                rest = (value - high.astype(jnp.float32)).astype(jnp.bfloat16)
                wide = jnp.concatenate([high, rest], 1)
                at, stop = wide_at[i], wide_at[i] + LANES + cross
                if fine_cross:
                    right = product(wide, table[:, at:stop])
                    right, turned = right[:, :LANES], right[:, LANES:]
                else:
                    turned = product(high, table[: 2 * GRID, at + LANES : stop])
                    right = None
                made.append((high, rest, wide, turned, right))
            solved = []
            for i, (high, rest, wide, turned, right) in enumerate(made):
                if not fine_cross:
                    right = product(wide, table[:, wide_at[i] : wide_at[i] + LANES])
                stack = [high, rest, high]
                for k in range(rank):
                    part = turned[:, LANES * k : LANES * (k + 1)]
                    part_high = part.astype(jnp.bfloat16)
                    stack.append(part_high)
                    if k < fine_cross:
                        stack += [(part - part_high.astype(jnp.float32)).astype(jnp.bfloat16), part_high]
                stack = jnp.concatenate([jnp.concatenate([p[r] for p in stack], 0) for r in rows], 1)
                left = product(table[GRID * i : GRID * (i + 1), left_at : left_at + stack.shape[0]], stack)
                left = jnp.concatenate([left[:, LANES * n : LANES * (n + 1)] for n in range(count)], 0)
                solved.append((right, left))
            return solved

        def react(state):
            sub, cat = state
            uptake = (h * sub) * (cat * cat)
            return sub + (supply - supply * sub - uptake), cat + (uptake - decay * cat)

        def step(state, extra=None):
            values = react(state)
            solved = solve(values)
            if extra is not None:
                values = plus(values, extra)
            return tuple((value + right) + left for value, (right, left) in zip(values, solved))

        def step_two(one, other):
            values = [jnp.concatenate(pair, 0) for pair in zip(react(one), react(other))]
            values = [(a + b) + c for a, (b, c) in zip(values, solve(values))]
            return tuple(v[:GRID] for v in values), tuple(v[GRID:] for v in values)

        step.two = step_two
        return step


FINE = Level(fine_step, 1, 0)
MIDDLE = Level(level_step, 1, 1)
COARSE = Level(coarse_step, 3, 1)
near_tables = np.concatenate([FINE.tables, MIDDLE.tables], 1)


def bound(fields, near_table, far_table=None):
    rates = loaded(fields.at[2:4])
    fine, middle = FINE.bind(near_table, 0, *rates), MIDDLE.bind(near_table, FINE.width, *rates)
    return fine, middle, None if far_table is None else COARSE.bind(far_table, 0, *rates)


def fetch_kernel(source, target):
    target[...] = source[...]


def relax_kernel(far_ref, fields, near_table, share_ref, arrived_ref):
    fine, middle, _ = bound(fields, near_table)
    position = lax.axis_index("tm")
    first = loaded(fields)
    prior = choose(position == 1, first, loaded(far_ref))
    for _ in range(STEPS_DEV):
        prior = fine(prior)
    shifted = choose(position == 0, first, prior)
    leap = middle(shifted)
    arrived = shifted
    for _ in range(STEPS_DEV):
        arrived = fine(arrived)
    share_ref[...] = merge(choose(position % GROUP == 0, shifted, minus(arrived, leap)))
    arrived_ref[...] = merge(arrived)


def chain(step, load, state, start, count, block):
    single = count % block

    def turn(j, state):
        return step(state, spread(load(j)))

    def turns(t, state):
        for i in range(block):
            state = turn(start + single + t * block + i, state)
        return state

    state = lax.fori_loop(start, start + single, turn, state) if not isinstance(single, int) or single else state
    return lax.fori_loop(0, count // block, turns, state)


def group_kernel(
    shares_ref, near_ref, arrived_ref, fields, near_table, far_table,
    first_ref, rhs_ref, parts_ref, residual_out, residual_ref, sems,
):
    fine, middle, coarse = bound(fields, near_table, far_table)
    position = lax.axis_index("tm")
    own = choose(position == 0, loaded(fields), loaded(near_ref))
    start = spread(shares_ref[0])
    state = start
    for _ in range(STEPS_DEV):
        state, own = fine.two(state, own)
    unpack_to(residual_ref, minus(spread(arrived_ref[...]), own))
    residual_copy = pltpu.make_async_copy(residual_ref, residual_out, sems.at[0])
    residual_copy.start()
    leap, handed = middle(start), coarse(start)
    first_ref[...] = merge(minus(state, leap))
    state = chain(middle, lambda j: shares_ref[j], state, 1, GROUP - 1, GROUP - 1)
    rhs = merge(choose(position < GROUP, state, minus(state, handed)))
    rhs_ref[...] = rhs
    part = jnp.where(position % 2 == 0, rhs[: GRID // 2], rhs[GRID // 2 :])
    for g in range(parts_ref.shape[0]):
        parts_ref[g] = part
    residual_copy.wait()


def correct_kernel(
    sides_ref, rhs_ref, shares_ref, first_ref, fields, near_table, far_table,
    points_ref, value_ref, defect_ref,
):
    fine, middle, coarse = bound(fields, near_table, far_table)
    position = lax.axis_index("tm")
    member, group_id = position % GROUP, position // GROUP

    def coarse_side(g):
        return jnp.concatenate([sides_ref[0, g], sides_ref[1, g]], 0)

    steps = jnp.maximum(group_id - 1, 0)
    earlier = chain(coarse, coarse_side, spread(coarse_side(0)), 1, steps, 10)
    earlier = choose(group_id == 0, loaded(fields), earlier)
    def right_side(j):
        return jnp.where(j == 0, first_ref[...], shares_ref[j])

    prior = chain(middle, right_side, earlier, 0, member, 3)
    updated = middle(prior, spread(right_side(member)))
    own_side = spread(rhs_ref[...])
    value = choose(group_id == 0, own_side, coarse(earlier, own_side))
    closing = member == GROUP - 1
    unpack_to(value_ref.at[0], value)
    unpack_to(points_ref.at[STEPS_DEV - 1], choose(closing, value, updated))
    unpack_to(defect_ref.at[0], choose(closing, minus(updated, value), minus(value, value)))
    state = prior
    for i in range(STEPS_DEV - 1):
        state = fine(state)
        unpack_to(points_ref.at[i], state)


VMEM = pl.BlockSpec(memory_space=pltpu.VMEM)
HBM = pl.BlockSpec(memory_space=pltpu.HBM)


def call(kernel, shapes, in_specs, out_specs, scratch, *operands):
    return pl.pallas_call(
        kernel,
        out_shape=[jax.ShapeDtypeStruct(s, jnp.float32) for s in shapes],
        in_specs=in_specs,
        out_specs=out_specs,
        scratch_shapes=scratch,
        compiler_params=pltpu.CompilerParams(vmem_limit_bytes=16 * 2**20),
    )(*operands)


def shards(initial, coarse_guess, feed_rate, kill_rate):
    devices = lax.axis_size("tm")
    groups = devices // GROUP
    field, pair, half = (GRID, LANES), (2, GRID, GRID), (GRID // 2, LANES)
    own = coarse_guess[0]
    far = lax.ppermute(own, "tm", [(i, i + 2) for i in range(devices - 2)])
    far_table = jnp.asarray(COARSE.tables)
    fields = jnp.concatenate([initial, feed_rate[None], kill_rate[None]], 0)
    near_table = pl.pallas_call(
        fetch_kernel,
        out_shape=jax.ShapeDtypeStruct(near_tables.shape, jnp.bfloat16),
        in_specs=[VMEM],
        out_specs=VMEM,
        cost_estimate=pl.CostEstimate(flops=0, bytes_accessed=4 * near_tables.size, transcendentals=0),
        compiler_params=pltpu.CompilerParams(vmem_limit_bytes=16 * 2**20),
    )(jnp.asarray(near_tables))
    near_table, own = lax.optimization_barrier((near_table, own))
    near = lax.ppermute(own, "tm", [(i, i + 1) for i in range(devices - 1)])
    share, arrived = call(relax_kernel, [field] * 2, [VMEM] * 3, [VMEM] * 2, [], far, fields, near_table)
    inside = [[g * GROUP + m for m in range(GROUP)] for g in range(groups)]
    shares = lax.all_gather(share, "tm", axis_index_groups=inside)
    parts_shape = (groups,) + half
    first, rhs, parts, residual = call(
        group_kernel,
        [field, field, parts_shape, pair],
        [VMEM] * 6,
        [VMEM] * 3 + [HBM],
        [pltpu.VMEM(pair, jnp.float32), pltpu.SemaphoreType.DMA((1,))],
        shares, near, arrived, fields, near_table, far_table,
    )
    across = [[g * GROUP + m for g in range(groups)] for m in range(GROUP)]
    parts = lax.all_to_all(parts, "tm", 0, 0, axis_index_groups=across)
    cores = [[2 * c, 2 * c + 1] for c in range(devices // 2)]
    sides = lax.all_gather(parts[: groups - 1], "tm", axis_index_groups=cores)
    points, value, defect = call(
        correct_kernel,
        [(STEPS_DEV,) + pair, (1,) + pair, (1,) + pair],
        [VMEM] * 7,
        [VMEM] * 3,
        [],
        sides, rhs, shares, first, fields, near_table, far_table,
    )
    return points, residual[None], value, defect


def solution(mesh):
    in_specs = (P(), P("tm", None, None, None), P(), P())
    out_specs = (P("tm", None, None, None),) * 4
    return jax.shard_map(shards, mesh=mesh, in_specs=in_specs, out_specs=out_specs, check_vma=False)
```

```python
import functools

import jax
import jax.numpy as jnp
import ml_dtypes
import numpy as np
from jax import lax
from jax.experimental import pallas as pl
from jax.experimental.pallas import tpu as pltpu
from jax.sharding import PartitionSpec as P

GRID = 64
GROUP = 16
STEPS_DEV = 4
LANES = 2 * GRID
diffusion = (0.2, 0.1)
interval_time = 0.03125
fine_step = interval_time / STEPS_DEV
level_step = interval_time
coarse_step = interval_time * GROUP


def basis_tables():
    positions = np.arange(GRID, dtype=np.float32)
    angles = np.float32(np.pi) * (positions[:, None] + np.float32(0.5)) * positions[None] / np.float32(GRID)
    weight = np.where(positions == 0, np.sqrt(np.float32(1 / GRID)), np.sqrt(np.float32(2 / GRID)))
    cosines = np.cos(angles.astype(np.float64)).astype(np.float32)
    basis = cosines * weight[None].astype(np.float32)
    sines = np.sin((np.float32(np.pi) * positions / np.float32(2 * GRID)).astype(np.float64)).astype(np.float32)
    return basis.astype(np.float64), (np.float32(-4) * sines * sines).astype(np.float64)


def solve_terms(time_step, rate, rank):
    basis, values = basis_tables()
    inverse = 1 / (1 - time_step * rate * (values[:, None] + values[None]))
    side = inverse[:, 0] - 1
    rest = inverse - 1 - side[:, None] - side[None]
    weights, vectors = np.linalg.eigh(rest)
    order = np.argsort(-np.abs(weights))[:rank]
    first = (basis * side) @ basis.T + basis @ basis.T - np.eye(GRID)
    cross = [(basis * (vectors[:, k] * np.sqrt(np.abs(weights[k])))) @ basis.T for k in order]
    return first, cross, [np.sign(weights[k]) for k in order]


def halves(matrix):
    high = matrix.astype(np.float32).astype(ml_dtypes.bfloat16)
    low = (matrix - high.astype(np.float64)).astype(np.float32).astype(ml_dtypes.bfloat16)
    return high, low


def twice(matrix):
    return np.concatenate([matrix, matrix], 1)


def species_tables(time_step, rate, rank, fine_cross):
    first, cross, signs = solve_terms(time_step, rate, rank)
    high, low = halves(first)
    right = np.concatenate([twice(high), twice(low), twice(high), np.zeros_like(twice(low))], 0)
    left = [high, high, low]
    cross_high, cross_low = zip(*[halves(m) for m in cross])
    cross_high = np.concatenate([twice(m) for m in cross_high], 1)
    cross_low = np.concatenate([twice(m) for m in cross_low], 1)
    parts = [cross_high, cross_low, cross_high] if fine_cross else [cross_high, cross_low]
    blank = np.zeros((4 * GRID - GRID * len(parts), cross_high.shape[1]), ml_dtypes.bfloat16)
    mixing = np.concatenate(parts + [blank], 0)
    for k, (matrix, sign) in enumerate(zip(cross, signs)):
        high, low = halves(matrix * sign)
        left += [high, high, low] if k < fine_cross else [high]
    return right, mixing, np.concatenate(left, 1)


@functools.lru_cache(None)
def level_tables(time_step, rank, fine_cross):
    sub = species_tables(time_step, diffusion[0], rank, fine_cross)
    cat = species_tables(time_step, diffusion[1], rank, fine_cross)
    left = np.concatenate([sub[2], cat[2]], 0)
    left = np.concatenate([left, np.zeros_like(left)], 0)
    return np.concatenate([sub[0], sub[1], cat[0], cat[1], left], 1)


def product(left, right):
    return jnp.dot(left, right, preferred_element_type=jnp.float32)


def second_half():
    return lax.broadcasted_iota(jnp.int32, (GRID, LANES), 1) >= GRID


def spread(fields):
    turned = pltpu.roll(fields, GRID, 1)
    second = second_half()
    return jnp.where(second, turned, fields), jnp.where(second, fields, turned)


def merge(state):
    return jnp.where(second_half(), state[1], state[0])


def loaded(pair):
    return tuple(jnp.concatenate([pair[i], pair[i]], 1) for i in range(2))


def unpack_to(ref, state):
    ref[0] = state[0][:, :GRID]
    ref[1] = state[1][:, :GRID]


def choose(condition, one, other):
    return tuple(jnp.where(condition, a, b) for a, b in zip(one, other))


def plus(one, other):
    return tuple(a + b for a, b in zip(one, other))


def minus(one, other):
    return tuple(a - b for a, b in zip(one, other))


class Level:
    def __init__(self, time_step, rank, fine_cross):
        self.time_step, self.rank, self.fine_cross = time_step, rank, fine_cross
        self.tables = level_tables(time_step, rank, fine_cross)
        self.width = self.tables.shape[1]

    def bind(self, table, start, feed, kill):
        h = jnp.float32(self.time_step)
        rank, fine_cross = self.rank, self.fine_cross
        cross = LANES * rank
        supply, decay = h * feed, h * (feed + kill)
        wide_at = [start, start + LANES + cross]
        left_at = start + 2 * (LANES + cross)
        order = (0, 1) if (rank, fine_cross) == (1, 1) else (1, 0)

        def solve(values):
            count = values[0].shape[0] // GRID
            rows = [slice(GRID * n, GRID * (n + 1)) for n in range(count)]
            made = []
            for i in order:
                value = values[i]
                high = value.astype(jnp.bfloat16)
                rest = (value - high.astype(jnp.float32)).astype(jnp.bfloat16)
                wide = jnp.concatenate([high, rest], 1)
                at, stop = wide_at[i], wide_at[i] + LANES + cross
                if fine_cross:
                    right = product(wide, table[:, at:stop])
                    right, turned = right[:, :LANES], right[:, LANES:]
                else:
                    turned = product(high, table[: 2 * GRID, at + LANES : stop])
                    right = None
                made.append((high, rest, wide, turned, right))
            solved = []
            for i, (high, rest, wide, turned, right) in zip(order, made):
                if not fine_cross:
                    right = product(wide, table[:, wide_at[i] : wide_at[i] + LANES])
                stack = [high, rest, high]
                for k in range(rank):
                    part = turned[:, LANES * k : LANES * (k + 1)]
                    part_high = part.astype(jnp.bfloat16)
                    stack.append(part_high)
                    if k < fine_cross:
                        stack += [(part - part_high.astype(jnp.float32)).astype(jnp.bfloat16), part_high]
                stack = jnp.concatenate([jnp.concatenate([p[r] for p in stack], 0) for r in rows], 1)
                left = product(table[GRID * i : GRID * (i + 1), left_at : left_at + stack.shape[0]], stack)
                left = jnp.concatenate([left[:, LANES * n : LANES * (n + 1)] for n in range(count)], 0)
                solved.append((right, left))
            return solved[:: order[1] - order[0]]

        def react(state):
            sub, cat = state
            uptake = (h * sub) * (cat * cat)
            return sub + (supply - supply * sub - uptake), cat + (uptake - decay * cat)

        def step(state, extra=None):
            values = react(state)
            solved = solve(values)
            if extra is not None:
                values = plus(values, extra)
            return tuple((value + right) + left for value, (right, left) in zip(values, solved))

        def step_two(one, other):
            values = [jnp.concatenate(pair, 0) for pair in zip(react(one), react(other))]
            values = [(a + b) + c for a, (b, c) in zip(values, solve(values))]
            return tuple(v[:GRID] for v in values), tuple(v[GRID:] for v in values)

        step.two = step_two
        return step


FINE = Level(fine_step, 1, 0)
MIDDLE = Level(level_step, 1, 1)
COARSE = Level(coarse_step, 3, 1)
near_tables = np.concatenate([FINE.tables, MIDDLE.tables], 1)


def bound(fields, near_table, far_table=None):
    rates = loaded(fields.at[2:4])
    fine, middle = FINE.bind(near_table, 0, *rates), MIDDLE.bind(near_table, FINE.width, *rates)
    return fine, middle, None if far_table is None else COARSE.bind(far_table, 0, *rates)


def fetch_kernel(source, target):
    target[...] = source[...]


def relax_kernel(far_ref, fields, near_table, share_ref, arrived_ref):
    fine, middle, _ = bound(fields, near_table)
    position = lax.axis_index("tm")
    first = loaded(fields)
    prior = choose(position == 1, first, loaded(far_ref))
    for _ in range(STEPS_DEV):
        prior = fine(prior)
    shifted = choose(position == 0, first, prior)
    leap = middle(shifted)
    arrived = shifted
    for _ in range(STEPS_DEV):
        arrived = fine(arrived)
    share_ref[...] = merge(choose(position % GROUP == 0, shifted, minus(arrived, leap)))
    arrived_ref[...] = merge(arrived)


def chain(step, load, state, start, count, block):
    single = count % block

    def turn(j, state):
        return step(state, spread(load(j)))

    def turns(t, state):
        for i in range(block):
            state = turn(start + single + t * block + i, state)
        return state

    state = lax.fori_loop(start, start + single, turn, state) if not isinstance(single, int) or single else state
    return lax.fori_loop(0, count // block, turns, state)


def group_kernel(
    shares_ref, near_ref, arrived_ref, fields, near_table, far_table,
    first_ref, rhs_ref, parts_ref, residual_out, residual_ref, sems,
):
    fine, middle, coarse = bound(fields, near_table, far_table)
    position = lax.axis_index("tm")
    own = choose(position == 0, loaded(fields), loaded(near_ref))
    start = spread(shares_ref[0])
    state = start
    for _ in range(STEPS_DEV):
        state, own = fine.two(state, own)
    unpack_to(residual_ref, minus(spread(arrived_ref[...]), own))
    residual_copy = pltpu.make_async_copy(residual_ref, residual_out, sems.at[0])
    residual_copy.start()
    leap, handed = middle(start), coarse(start)
    first_ref[...] = merge(minus(state, leap))
    state = chain(middle, lambda j: shares_ref[j], state, 1, GROUP - 1, GROUP - 1)
    rhs = merge(choose(position < GROUP, state, minus(state, handed)))
    rhs_ref[...] = rhs
    part = jnp.where(position % 2 == 0, rhs[: GRID // 2], rhs[GRID // 2 :])
    for g in range(parts_ref.shape[0]):
        parts_ref[g] = part
    residual_copy.wait()


def correct_kernel(
    sides_ref, rhs_ref, shares_ref, first_ref, fields, near_table, far_table,
    points_out, value_out, defect_out, points_ref, value_ref, defect_ref, sems,
):
    fine, middle, coarse = bound(fields, near_table, far_table)
    position = lax.axis_index("tm")
    member, group_id = position % GROUP, position // GROUP

    def coarse_side(g):
        return jnp.concatenate([sides_ref[0, g], sides_ref[1, g]], 0)

    steps = jnp.maximum(group_id - 1, 0)
    earlier = chain(coarse, coarse_side, spread(coarse_side(0)), 1, steps, 10)
    earlier = choose(group_id == 0, loaded(fields), earlier)
    copies = []

    def emit(source, target):
        copies.append(pltpu.make_async_copy(source, target, sems.at[len(copies)]))
        copies[-1].start()

    def right_side(j):
        return jnp.where(j == 0, first_ref[...], shares_ref[j])

    prior = chain(middle, right_side, earlier, 0, member, 3)
    updated = middle(prior, spread(right_side(member)))
    own_side = spread(rhs_ref[...])
    value = choose(group_id == 0, own_side, coarse(earlier, own_side))
    closing = member == GROUP - 1
    state = prior
    for i in range(STEPS_DEV - 1):
        state = fine(state)
        unpack_to(points_ref.at[i], state)
        emit(points_ref.at[i], points_out.at[i])
        if i == 0:
            unpack_to(value_ref, value)
            emit(value_ref, value_out.at[0])
            unpack_to(points_ref.at[STEPS_DEV - 1], choose(closing, value, updated))
            emit(points_ref.at[STEPS_DEV - 1], points_out.at[STEPS_DEV - 1])
            unpack_to(defect_ref, choose(closing, minus(updated, value), minus(value, value)))
            emit(defect_ref, defect_out.at[0])
    for copy in copies:
        copy.wait()


VMEM = pl.BlockSpec(memory_space=pltpu.VMEM)
HBM = pl.BlockSpec(memory_space=pltpu.HBM)


def call(kernel, shapes, in_specs, out_specs, scratch, *operands):
    return pl.pallas_call(
        kernel,
        out_shape=[jax.ShapeDtypeStruct(s, jnp.float32) for s in shapes],
        in_specs=in_specs,
        out_specs=out_specs,
        scratch_shapes=scratch,
        compiler_params=pltpu.CompilerParams(vmem_limit_bytes=16 * 2**20),
    )(*operands)


def shards(initial, coarse_guess, feed_rate, kill_rate):
    devices = lax.axis_size("tm")
    groups = devices // GROUP
    field, pair, half = (GRID, LANES), (2, GRID, GRID), (GRID // 2, LANES)
    own = coarse_guess[0]
    far = lax.ppermute(own, "tm", [(i, i + 2) for i in range(devices - 2)])
    far_table = jnp.asarray(COARSE.tables)
    fields = jnp.concatenate([initial, feed_rate[None], kill_rate[None]], 0)
    near_table = pl.pallas_call(
        fetch_kernel,
        out_shape=jax.ShapeDtypeStruct(near_tables.shape, jnp.bfloat16),
        in_specs=[VMEM],
        out_specs=VMEM,
        cost_estimate=pl.CostEstimate(flops=0, bytes_accessed=4 * near_tables.size, transcendentals=0),
        compiler_params=pltpu.CompilerParams(vmem_limit_bytes=16 * 2**20),
    )(jnp.asarray(near_tables))
    near_table, own = lax.optimization_barrier((near_table, own))
    near = lax.ppermute(own, "tm", [(i, i + 1) for i in range(devices - 1)])
    share, arrived = call(relax_kernel, [field] * 2, [VMEM] * 3, [VMEM] * 2, [], far, fields, near_table)
    inside = [[g * GROUP + m for m in range(GROUP)] for g in range(groups)]
    shares = lax.all_gather(share, "tm", axis_index_groups=inside)
    parts_shape = (groups,) + half
    first, rhs, parts, residual = call(
        group_kernel,
        [field, field, parts_shape, pair],
        [VMEM] * 6,
        [VMEM] * 3 + [HBM],
        [pltpu.VMEM(pair, jnp.float32), pltpu.SemaphoreType.DMA((1,))],
        shares, near, arrived, fields, near_table, far_table,
    )
    across = [[g * GROUP + m for g in range(groups)] for m in range(GROUP)]
    parts = lax.all_to_all(parts, "tm", 0, 0, axis_index_groups=across)
    cores = [[2 * c, 2 * c + 1] for c in range(devices // 2)]
    sides = lax.all_gather(parts[: groups - 1], "tm", axis_index_groups=cores)
    shapes = [(STEPS_DEV,) + pair, pair, pair]
    points, value, defect = call(
        correct_kernel,
        [(STEPS_DEV,) + pair, (1,) + pair, (1,) + pair],
        [VMEM] * 7,
        [HBM] * 3,
        [pltpu.VMEM(s, jnp.float32) for s in shapes] + [pltpu.SemaphoreType.DMA((STEPS_DEV + 2,))],
        sides, rhs, shares, first, fields, near_table, far_table,
    )
    return points, residual[None], value, defect


def solution(mesh):
    in_specs = (P(), P("tm", None, None, None), P(), P())
    out_specs = (P("tm", None, None, None),) * 4
    return jax.shard_map(shards, mesh=mesh, in_specs=in_specs, out_specs=out_specs, check_vma=False)
```

```python
import functools

import jax
import jax.numpy as jnp
import ml_dtypes
import numpy as np
from jax import lax
from jax.experimental import pallas as pl
from jax.experimental.pallas import tpu as pltpu
from jax.sharding import PartitionSpec as P

GRID = 64
GROUP = 16
STEPS_DEV = 4
LANES = 2 * GRID
diffusion = (0.2, 0.1)
interval_time = 0.03125
fine_step = interval_time / STEPS_DEV
level_step = interval_time
coarse_step = interval_time * GROUP


def basis_tables():
    positions = np.arange(GRID, dtype=np.float32)
    angles = np.float32(np.pi) * (positions[:, None] + np.float32(0.5)) * positions[None] / np.float32(GRID)
    weight = np.where(positions == 0, np.sqrt(np.float32(1 / GRID)), np.sqrt(np.float32(2 / GRID)))
    cosines = np.cos(angles.astype(np.float64)).astype(np.float32)
    basis = cosines * weight[None].astype(np.float32)
    sines = np.sin((np.float32(np.pi) * positions / np.float32(2 * GRID)).astype(np.float64)).astype(np.float32)
    return basis.astype(np.float64), (np.float32(-4) * sines * sines).astype(np.float64)


def solve_terms(time_step, rate, rank):
    basis, values = basis_tables()
    inverse = 1 / (1 - time_step * rate * (values[:, None] + values[None]))
    side = inverse[:, 0] - 1
    rest = inverse - 1 - side[:, None] - side[None]
    weights, vectors = np.linalg.eigh(rest)
    order = np.argsort(-np.abs(weights))[:rank]
    first = (basis * side) @ basis.T + basis @ basis.T - np.eye(GRID)
    cross = [(basis * (vectors[:, k] * np.sqrt(np.abs(weights[k])))) @ basis.T for k in order]
    return first, cross, [np.sign(weights[k]) for k in order]


def halves(matrix):
    high = matrix.astype(np.float32).astype(ml_dtypes.bfloat16)
    low = (matrix - high.astype(np.float64)).astype(np.float32).astype(ml_dtypes.bfloat16)
    return high, low


def twice(matrix):
    return np.concatenate([matrix, matrix], 1)


def species_tables(time_step, rate, rank, fine_cross):
    first, cross, signs = solve_terms(time_step, rate, rank)
    high, low = halves(first)
    right = np.concatenate([twice(high), twice(low), twice(high), np.zeros_like(twice(low))], 0)
    left = [high, high, low]
    cross_high, cross_low = zip(*[halves(m) for m in cross])
    cross_high = np.concatenate([twice(m) for m in cross_high], 1)
    cross_low = np.concatenate([twice(m) for m in cross_low], 1)
    parts = [cross_high, cross_low, cross_high] if fine_cross else [cross_high, cross_low]
    blank = np.zeros((4 * GRID - GRID * len(parts), cross_high.shape[1]), ml_dtypes.bfloat16)
    mixing = np.concatenate(parts + [blank], 0)
    for k, (matrix, sign) in enumerate(zip(cross, signs)):
        high, low = halves(matrix * sign)
        left += [high, high, low] if k < fine_cross else [high]
    return right, mixing, np.concatenate(left, 1)


@functools.lru_cache(None)
def level_tables(time_step, rank, fine_cross):
    sub = species_tables(time_step, diffusion[0], rank, fine_cross)
    cat = species_tables(time_step, diffusion[1], rank, fine_cross)
    left = np.concatenate([sub[2], cat[2]], 0)
    left = np.concatenate([left, np.zeros_like(left)], 0)
    return np.concatenate([sub[0], sub[1], cat[0], cat[1], left], 1)


def product(left, right):
    return jnp.dot(left, right, preferred_element_type=jnp.float32)


def second_half():
    return lax.broadcasted_iota(jnp.int32, (GRID, LANES), 1) >= GRID


def spread(fields):
    turned = pltpu.roll(fields, GRID, 1)
    second = second_half()
    return jnp.where(second, turned, fields), jnp.where(second, fields, turned)


def merge(state):
    return jnp.where(second_half(), state[1], state[0])


def loaded(pair):
    return tuple(jnp.concatenate([pair[i], pair[i]], 1) for i in range(2))


def unpack_to(ref, state):
    ref[0] = state[0][:, :GRID]
    ref[1] = state[1][:, :GRID]


def choose(condition, one, other):
    return tuple(jnp.where(condition, a, b) for a, b in zip(one, other))


def plus(one, other):
    return tuple(a + b for a, b in zip(one, other))


def minus(one, other):
    return tuple(a - b for a, b in zip(one, other))


class Level:
    def __init__(self, time_step, rank, fine_cross):
        self.time_step, self.rank, self.fine_cross = time_step, rank, fine_cross
        self.tables = level_tables(time_step, rank, fine_cross)
        self.width = self.tables.shape[1]

    def bind(self, table, start, feed, kill):
        h = jnp.float32(self.time_step)
        rank, fine_cross = self.rank, self.fine_cross
        cross = LANES * rank
        supply, decay = h * feed, h * (feed + kill)
        wide_at = [start, start + LANES + cross]
        left_at = start + 2 * (LANES + cross)

        def solve(values):
            count = values[0].shape[0] // GRID
            rows = [slice(GRID * n, GRID * (n + 1)) for n in range(count)]
            made = []
            for i, value in enumerate(values):
                high = value.astype(jnp.bfloat16)
                rest = (value - high.astype(jnp.float32)).astype(jnp.bfloat16)
                wide = jnp.concatenate([high, rest], 1)
                at, stop = wide_at[i], wide_at[i] + LANES + cross
                if fine_cross:
                    right = product(wide, table[:, at:stop])
                    right, turned = right[:, :LANES], right[:, LANES:]
                else:
                    turned = product(high, table[: 2 * GRID, at + LANES : stop])
                    right = None
                made.append((high, rest, wide, turned, right))
            solved = []
            for i, (high, rest, wide, turned, right) in enumerate(made):
                if not fine_cross:
                    right = product(wide, table[:, wide_at[i] : wide_at[i] + LANES])
                stack = [high, rest, high]
                for k in range(rank):
                    part = turned[:, LANES * k : LANES * (k + 1)]
                    part_high = part.astype(jnp.bfloat16)
                    stack.append(part_high)
                    if k < fine_cross:
                        stack += [(part - part_high.astype(jnp.float32)).astype(jnp.bfloat16), part_high]
                stack = jnp.concatenate([jnp.concatenate([p[r] for p in stack], 0) for r in rows], 1)
                left = product(table[GRID * i : GRID * (i + 1), left_at : left_at + stack.shape[0]], stack)
                left = jnp.concatenate([left[:, LANES * n : LANES * (n + 1)] for n in range(count)], 0)
                solved.append((right, left))
            return solved

        def react(state):
            sub, cat = state
            uptake = (h * sub) * (cat * cat)
            return sub + (supply - supply * sub - uptake), cat + (uptake - decay * cat)

        def step(state, extra=None):
            values = react(state)
            solved = solve(values)
            if extra is not None:
                values = plus(values, extra)
            return tuple((value + right) + left for value, (right, left) in zip(values, solved))

        def step_two(one, other):
            values = [jnp.concatenate(pair, 0) for pair in zip(react(one), react(other))]
            values = [(a + b) + c for a, (b, c) in zip(values, solve(values))]
            return tuple(v[:GRID] for v in values), tuple(v[GRID:] for v in values)

        step.two = step_two
        return step


FINE = Level(fine_step, 1, 0)
MIDDLE = Level(level_step, 1, 1)
COARSE = Level(coarse_step, 3, 1)
near_tables = np.concatenate([FINE.tables, MIDDLE.tables], 1)


def bound(fields, near_table, far_table=None):
    rates = loaded(fields.at[2:4])
    fine, middle = FINE.bind(near_table, 0, *rates), MIDDLE.bind(near_table, FINE.width, *rates)
    return fine, middle, None if far_table is None else COARSE.bind(far_table, 0, *rates)


def fetch_kernel(source, target):
    target[...] = source[...]


def relax_kernel(far_ref, fields, near_table, share_ref, arrived_ref):
    fine, middle, _ = bound(fields, near_table)
    position = lax.axis_index("tm")
    first = loaded(fields)
    prior = choose(position == 1, first, loaded(far_ref))
    for _ in range(STEPS_DEV):
        prior = fine(prior)
    shifted = choose(position == 0, first, prior)
    leap = middle(shifted)
    arrived = shifted
    for _ in range(STEPS_DEV):
        arrived = fine(arrived)
    share_ref[...] = merge(choose(position % GROUP == 0, shifted, minus(arrived, leap)))
    arrived_ref[...] = merge(arrived)


def chain(step, load, state, start, count, block):
    single = count % block

    def turn(j, state):
        return step(state, spread(load(j)))

    def turns(t, state):
        for i in range(block):
            state = turn(start + single + t * block + i, state)
        return state

    state = lax.fori_loop(start, start + single, turn, state) if not isinstance(single, int) or single else state
    return turns(0, state) if isinstance(count, int) and count == block else lax.fori_loop(0, count // block, turns, state)


def group_kernel(
    shares_ref, near_ref, arrived_ref, fields, near_table, far_table,
    first_ref, rhs_ref, parts_ref, residual_out, residual_ref, sems,
):
    fine, middle, coarse = bound(fields, near_table, far_table)
    position = lax.axis_index("tm")
    own = choose(position == 0, loaded(fields), loaded(near_ref))
    start = spread(shares_ref[0])
    state = start
    for _ in range(STEPS_DEV):
        state, own = fine.two(state, own)
    unpack_to(residual_ref, minus(spread(arrived_ref[...]), own))
    residual_copy = pltpu.make_async_copy(residual_ref, residual_out, sems.at[0])
    residual_copy.start()
    leap, handed = middle(start), coarse(start)
    first_ref[...] = merge(minus(state, leap))
    state = chain(middle, lambda j: shares_ref[j], state, 1, GROUP - 1, GROUP - 1)
    rhs = merge(choose(position < GROUP, state, minus(state, handed)))
    rhs_ref[...] = rhs
    part = jnp.where(position % 2 == 0, rhs[: GRID // 2], rhs[GRID // 2 :])
    for g in range(parts_ref.shape[0]):
        parts_ref[g] = part
    residual_copy.wait()


def correct_kernel(
    sides_ref, rhs_ref, shares_ref, first_ref, fields, near_table, far_table,
    points_out, value_out, defect_out, points_ref, value_ref, defect_ref, sems,
):
    fine, middle, coarse = bound(fields, near_table, far_table)
    position = lax.axis_index("tm")
    member, group_id = position % GROUP, position // GROUP

    def coarse_side(g):
        return jnp.concatenate([sides_ref[0, g], sides_ref[1, g]], 0)

    steps = jnp.maximum(group_id - 1, 0)
    earlier = chain(coarse, coarse_side, spread(coarse_side(0)), 1, steps, 10)
    earlier = choose(group_id == 0, loaded(fields), earlier)
    copies = []

    def emit(source, target):
        copies.append(pltpu.make_async_copy(source, target, sems.at[len(copies)]))
        copies[-1].start()

    def right_side(j):
        return jnp.where(j == 0, first_ref[...], shares_ref[j])

    prior = chain(middle, right_side, earlier, 0, member, 3)
    updated = middle(prior, spread(right_side(member)))
    own_side = spread(rhs_ref[...])
    value = choose(group_id == 0, own_side, coarse(earlier, own_side))
    closing = member == GROUP - 1
    state = prior
    for i in range(STEPS_DEV - 1):
        state = fine(state)
        unpack_to(points_ref.at[i], state)
        emit(points_ref.at[i], points_out.at[i])
        if i == 0:
            unpack_to(value_ref, value)
            emit(value_ref, value_out.at[0])
            unpack_to(points_ref.at[STEPS_DEV - 1], choose(closing, value, updated))
            emit(points_ref.at[STEPS_DEV - 1], points_out.at[STEPS_DEV - 1])
            unpack_to(defect_ref, choose(closing, minus(updated, value), minus(value, value)))
            emit(defect_ref, defect_out.at[0])
    for copy in copies:
        copy.wait()


VMEM = pl.BlockSpec(memory_space=pltpu.VMEM)
HBM = pl.BlockSpec(memory_space=pltpu.HBM)


def call(kernel, shapes, in_specs, out_specs, scratch, *operands):
    return pl.pallas_call(
        kernel,
        out_shape=[jax.ShapeDtypeStruct(s, jnp.float32) for s in shapes],
        in_specs=in_specs,
        out_specs=out_specs,
        scratch_shapes=scratch,
        compiler_params=pltpu.CompilerParams(vmem_limit_bytes=16 * 2**20),
    )(*operands)


def shards(initial, coarse_guess, feed_rate, kill_rate):
    devices = lax.axis_size("tm")
    groups = devices // GROUP
    field, pair, half = (GRID, LANES), (2, GRID, GRID), (GRID // 2, LANES)
    own = coarse_guess[0]
    far = lax.ppermute(own, "tm", [(i, i + 2) for i in range(devices - 2)])
    far_table = jnp.asarray(COARSE.tables)
    fields = jnp.concatenate([initial, feed_rate[None], kill_rate[None]], 0)
    near_table = pl.pallas_call(
        fetch_kernel,
        out_shape=jax.ShapeDtypeStruct(near_tables.shape, jnp.bfloat16),
        in_specs=[VMEM],
        out_specs=VMEM,
        cost_estimate=pl.CostEstimate(flops=0, bytes_accessed=4 * near_tables.size, transcendentals=0),
        compiler_params=pltpu.CompilerParams(vmem_limit_bytes=16 * 2**20),
    )(jnp.asarray(near_tables))
    near_table, own = lax.optimization_barrier((near_table, own))
    near = lax.ppermute(own, "tm", [(i, i + 1) for i in range(devices - 1)])
    share, arrived = call(relax_kernel, [field] * 2, [VMEM] * 3, [VMEM] * 2, [], far, fields, near_table)
    inside = [[g * GROUP + m for m in range(GROUP)] for g in range(groups)]
    shares = lax.all_gather(share, "tm", axis_index_groups=inside)
    parts_shape = (groups,) + half
    first, rhs, parts, residual = call(
        group_kernel,
        [field, field, parts_shape, pair],
        [VMEM] * 6,
        [VMEM] * 3 + [HBM],
        [pltpu.VMEM(pair, jnp.float32), pltpu.SemaphoreType.DMA((1,))],
        shares, near, arrived, fields, near_table, far_table,
    )
    across = [[g * GROUP + m for g in range(groups)] for m in range(GROUP)]
    parts = lax.all_to_all(parts, "tm", 0, 0, axis_index_groups=across)
    cores = [[2 * c, 2 * c + 1] for c in range(devices // 2)]
    sides = lax.all_gather(parts[: groups - 1], "tm", axis_index_groups=cores)
    shapes = [(STEPS_DEV,) + pair, pair, pair]
    points, value, defect = call(
        correct_kernel,
        [(STEPS_DEV,) + pair, (1,) + pair, (1,) + pair],
        [VMEM] * 7,
        [HBM] * 3,
        [pltpu.VMEM(s, jnp.float32) for s in shapes] + [pltpu.SemaphoreType.DMA((STEPS_DEV + 2,))],
        sides, rhs, shares, first, fields, near_table, far_table,
    )
    return points, residual[None], value, defect


def solution(mesh):
    in_specs = (P(), P("tm", None, None, None), P(), P())
    out_specs = (P("tm", None, None, None),) * 4
    return jax.shard_map(shards, mesh=mesh, in_specs=in_specs, out_specs=out_specs, check_vma=False)
```
